256 devices in a mesh: step: 8 (over x, core), frame: 32 (over z, y).
Axes of the slice: x: 4, y: 4, z: 8, core: 2. Of those that a mesh axis runs over, the one named last changes fastest.
Arguments:
- latents: bfloat16 [8, 8192, 1536], P('step', 'frame')
- anchor: float32 [8192, 1536], P('frame'), may hold values from -6 to 6
- step_index: int32 [8], replicated, may hold values from 0 to 49, as said below
- modulation: float32 [50, 3, 1536], replicated, may hold values from -3 to 3
- step_sizes: float32 [50], replicated, may hold values from 0.02 to 0.2
- input_weight: bfloat16 [1536, 2304], P(('step', 'frame'))
- output_weight: bfloat16 [768, 1536], P(('step', 'frame')), may hold values from -0.21875 to 0.21875
- norm_gain: float32 [2, 768], replicated, may hold values from 1 to 8, as said below
- block_mask: int32 [64, 64], P('frame'), may hold values from 0 to 1, as said below
Outputs:
- velocity: bfloat16 [8, 8192, 1536], P('step', 'frame')
- advanced: float32 [8, 8192, 1536], P('step', 'frame')
The draws below stay inside these ranges and needn't reach their ends.
Inputs may be any that keep to these rules, and one draw needn't show every extreme that they name: `step_index`: the 8 values are distinct; 0 and 49 are always among them. `norm_gain`: positive. A frame slab is 2 consecutive blocks. block_mask[b, b] = 1 for every block b, and block_mask[a, b] = 0 unless the slabs of a and b are equal or a power of two apart.
All inputs are finite; a program needn't handle non-finite values.
Results may differ from the reference program's by a relative error of at most 0.0068.
Values may be sent and summed in bfloat16 or wider, within the bound.
No kernel may reach another device: no remote copies, remote signals or barrier semaphores. Data moves between devices by JAX's collectives and lax.ppermute only.
A program may use at most 64 MiB of HBM per device.

```python
import math
import jax
import jax.numpy as jnp
from jax import lax

D = 1536
HEADS = 6
HD = 128
BLK = 128
NSCHED = 50
TOK_DEV = 256
HQ = 768
BLOCKS_DEV = 2
STEPS = 8
TOKENS = 8192
NBLK = 64
N_FRAME = 32


def draw_latents(key, part):
    key = jax.random.fold_in(key, 11)
    base_key = jax.random.fold_in(key, 0)
    return jnp.clip(jax.random.normal(base_key, (STEPS, TOKENS, D), jnp.float32), -6.0, 6.0).astype(jnp.bfloat16)


def draw_step_index(key, part):
    key = jax.random.fold_in(key, 23)
    middle_key, order_key = jax.random.split(key)
    middle = jax.random.permutation(middle_key, NSCHED - 2)[:STEPS - 2].astype(jnp.int32) + 1
    ends = jnp.array([0, NSCHED - 1], dtype=jnp.int32)
    values = jnp.concatenate([ends, middle])
    order = jax.random.permutation(order_key, STEPS)
    return values[order].astype(jnp.int32)


def draw_input_weight(key, part):
    key = jax.random.fold_in(key, 37)
    weight_scale = 1.0 / math.sqrt(D)
    entries = jnp.clip(jax.random.normal(key, (D, 3 * HQ), jnp.float32), -4.0, 4.0) * weight_scale
    return entries.astype(jnp.bfloat16)


def draw_norm_gain(key, part):
    key = jax.random.fold_in(key, 41)
    jitter_key = jax.random.fold_in(key, 0)
    return jax.random.uniform(jitter_key, (2, HQ), jnp.float32, 1.0, 2.0)


def draw_block_mask(key, part):
    key = jax.random.fold_in(key, 53)
    block_ids = jnp.arange(NBLK, dtype=jnp.int32)
    slab_ids = block_ids // BLOCKS_DEV
    slab_gap = jnp.abs(slab_ids[:, None] - slab_ids[None, :])
    power_gap = jnp.logical_and(slab_gap > 0, jnp.bitwise_and(slab_gap, slab_gap - 1) == 0)
    coin_flip = jax.random.randint(key, (NBLK, NBLK), 0, 4)
    live_pair = jnp.where(slab_gap == 0, coin_flip < 3, jnp.logical_and(power_gap, coin_flip < 2))
    live_pair = jnp.logical_or(live_pair, block_ids[:, None] == block_ids[None, :])
    return live_pair.astype(jnp.int32)


def level_of(rng, extent, cuts, least, largest):
    def one(position, shards_of):
        draws = jax.random.uniform(jax.random.fold_in(jax.random.fold_in(rng, 6), position), (shards_of,), jnp.float32, least / len(cuts), largest / len(cuts))
        return jnp.repeat(jnp.exp(draws), extent[position] // shards_of).reshape((-1,) + (1,) * (len(extent) - position - 1))

    level = one(*cuts[0])
    for cut in cuts[1:]:
        level = level * one(*cut)
    return level


def normal_values(rng, extent, deviation, limit, shards=(), held_as=jnp.bfloat16):
    drawn = deviation * jax.random.normal(rng, extent, jnp.float32)
    if shards:
        drawn = drawn * level_of(rng, extent, shards, -0.22, 0.18)
    return jnp.clip(drawn, -limit, limit).astype(held_as)


def setup_inputs(seed: int = 0) -> dict:
    key_of = jax.random.split(jax.random.key(seed), 10)
    return {
        "latents": draw_latents(jax.random.fold_in(key_of[9], 71), 0),
        "anchor": normal_values(key_of[1], (TOKENS, D), 1.0, 6.0, ((0, 32),), jnp.float32),
        "step_index": draw_step_index(jax.random.fold_in(key_of[9], 71), 0),
        "modulation": normal_values(key_of[3], (NSCHED, 3, D), 0.5, 3.0, (), jnp.float32),
        "step_sizes": jnp.clip(jnp.exp(jax.random.uniform(key_of[4], (NSCHED,), jnp.float32, math.log(0.02), math.log(0.2))), 0.02, 0.2),
        "input_weight": draw_input_weight(jax.random.fold_in(key_of[9], 71), 0),
        "output_weight": normal_values(key_of[6], (HQ, D), HQ ** -0.5, 0.21875, ((0, 256),)),
        "norm_gain": draw_norm_gain(jax.random.fold_in(key_of[9], 71), 0),
        "block_mask": draw_block_mask(jax.random.fold_in(key_of[9], 71), 0),
    }


norm_eps = 1e-06

def layer_norm(inputs):
    row_mean = lax.optimization_barrier(jnp.mean(inputs, axis=-1, keepdims=True))
    centered = inputs - row_mean
    variance = lax.optimization_barrier(jnp.mean(centered * centered, axis=-1, keepdims=True))
    return centered * lax.rsqrt(variance + norm_eps)

def rms_norm(inputs, gain_row):
    square = lax.optimization_barrier(jnp.mean(inputs * inputs, axis=-1, keepdims=True))
    return inputs * lax.rsqrt(square + norm_eps) * gain_row

def group_velocity(latent, own_index, modulation, step_sizes, input_weight, output_weight, norm_gain, block_mask):
    one_hot = (jnp.arange(NSCHED, dtype=jnp.int32) == own_index).astype(jnp.float32)
    modulation_row = lax.optimization_barrier(jnp.sum(one_hot[:, None, None] * modulation, axis=0))
    group_size = jnp.sum(one_hot * step_sizes)
    normed = layer_norm(latent.astype(jnp.float32))
    modulated = (normed * (1.0 + modulation_row[1]) + modulation_row[0]).astype(jnp.bfloat16)
    projected = jnp.dot(modulated, input_weight, preferred_element_type=jnp.float32)
    queries = rms_norm(projected[:, :HQ], norm_gain[0]).astype(jnp.bfloat16)
    key_rows = rms_norm(projected[:, HQ:2 * HQ], norm_gain[1]).astype(jnp.bfloat16)
    value_rows = projected[:, 2 * HQ:].astype(jnp.bfloat16)
    key_heads = lax.optimization_barrier(key_rows).astype(jnp.float32).reshape(TOKENS, HEADS, HD)
    value_heads = lax.optimization_barrier(value_rows).astype(jnp.float32).reshape(TOKENS, HEADS, HD)
    query_float = lax.optimization_barrier(queries).astype(jnp.float32)
    slab_queries = query_float.reshape(N_FRAME, TOK_DEV, HEADS, HD)
    slab_masks = block_mask.reshape(N_FRAME, BLOCKS_DEV, NBLK)
    score_scale = 1.0 / math.sqrt(HD)

    def one_slab(slab_args):
        query_block, mask_block = slab_args
        allowed = jnp.repeat(jnp.repeat(mask_block > 0, BLK, axis=0), BLK, axis=1)
        scores = jnp.einsum('qhd,khd->hqk', query_block, key_heads) * score_scale
        scores = jnp.where(allowed[None], scores, -jnp.inf)
        row_peak = lax.optimization_barrier(jnp.max(scores, axis=-1, keepdims=True))
        exp_terms = jnp.exp(scores - row_peak)
        row_total = lax.optimization_barrier(jnp.sum(exp_terms, axis=-1, keepdims=True))
        rounded = lax.optimization_barrier(exp_terms.astype(jnp.bfloat16)).astype(jnp.float32)
        mixed_block = jnp.einsum('hqk,khd->qhd', rounded, value_heads) / jnp.transpose(row_total, (1, 0, 2))
        return mixed_block.reshape(TOK_DEV, HQ).astype(jnp.bfloat16)
    mixed = lax.map(one_slab, (slab_queries, slab_masks)).reshape(TOKENS, HQ)
    output_rows = jnp.dot(mixed, output_weight, preferred_element_type=jnp.float32)
    velocity = (modulation_row[2] * output_rows).astype(jnp.bfloat16)
    return (velocity, group_size)

def reference(latents, anchor, step_index, modulation, step_sizes, input_weight, output_weight, norm_gain, block_mask):

    def per_group(group_args):
        latent, own_index = group_args
        return group_velocity(latent, own_index, modulation, step_sizes, input_weight, output_weight, norm_gain, block_mask)
    velocity, group_sizes = lax.map(per_group, (latents, step_index))
    weighted = group_sizes[:, None, None] * velocity.astype(jnp.float32)
    advanced = anchor[None] + jnp.cumsum(weighted, axis=0)
    return (velocity, advanced)
```

```python
import functools
import math

import jax
import jax.numpy as jnp
from jax import lax
from jax.experimental import pallas as pl
from jax.experimental.pallas import tpu as pltpu
from jax.sharding import PartitionSpec as P

HD = 128
BLK = 128
NX, NY, NZ = 4, 4, 8
NORM_EPS = 1e-06
F32 = jnp.float32
BF16 = jnp.bfloat16
VMEM_LIMIT = 56 * 1024 * 1024


def y_shift(block, distance):
    pairs = [(4 * z + y, 4 * z + (y + distance) % NY) for z in range(NZ) for y in range(NY)]
    return lax.ppermute(block, "frame", pairs)


def z_shift(block, distance):
    pairs = [(4 * z + y, 4 * ((z + distance) % NZ) + y) for z in range(NZ) for y in range(NY)]
    return lax.ppermute(block, "frame", pairs)


def x_shift(block, distance):
    pairs = [(2 * x + c, 2 * ((x + distance) % NX) + c) for x in range(NX) for c in range(2)]
    return lax.ppermute(block, "step", pairs)


def x_later(block, distance):
    pairs = [(2 * x + c, 2 * (x + distance) + c) for x in range(NX - distance) for c in range(2)]
    return lax.ppermute(block, "step", pairs)


def core_swap(block):
    return lax.ppermute(block, "step", [(i, i ^ 1) for i in range(2 * NX)])


def modulate_kernel(where_ref, index_ref, latent_ref, row_ref, out_ref):
    value = latent_ref[...].astype(F32)
    centered = value - jnp.mean(value, axis=-1, keepdims=True)
    variance = jnp.mean(centered * centered, axis=-1, keepdims=True)
    normed = centered * lax.rsqrt(variance + NORM_EPS)
    out_ref[...] = (normed * (1.0 + row_ref[0, 1:2, :]) + row_ref[0, 0:1, :]).astype(BF16)


def modulate(where, step_index, latent, modulation):
    rows, width = latent.shape
    return pl.pallas_call(
        modulate_kernel,
        grid_spec=pltpu.PrefetchScalarGridSpec(
            num_scalar_prefetch=2,
            grid=(2,),
            in_specs=[
                pl.BlockSpec((rows // 2, width), lambda i, w, s: (i, 0)),
                pl.BlockSpec((1, 3, width), lambda i, w, s: (s[w[0]], 0, 0)),
            ],
            out_specs=pl.BlockSpec((rows // 2, width), lambda i, w, s: (i, 0)),
        ),
        out_shape=jax.ShapeDtypeStruct((rows, width), BF16),
        name="modulate",
    )(where, step_index, latent, modulation)


N_SLABS = 10


def attend_kernel(
    where_ref,
    mask_ref,
    gain_ref,
    *refs,
):
    slabs = refs[:9]
    z4_top, z4_bottom = refs[9:11]
    pieces = refs[11:21]
    out_ref = refs[21]
    m_s, w_s, k_s, v_s, q_s, bias_s, m_sem, w_sem = refs[22:]
    x, core, frame = where_ref[1], where_ref[2], where_ref[3]
    rows = q_s.shape[0]
    feats = q_s.shape[1]
    half = rows // 2

    copies_m = []
    for i in range(9):
        copies_m.append(pltpu.make_async_copy(slabs[i], m_s.at[pl.ds(i * rows, rows)], m_sem.at[i]))
    copies_m.append(pltpu.make_async_copy(z4_top, m_s.at[pl.ds(9 * rows, half)], m_sem.at[9]))
    copies_m.append(
        pltpu.make_async_copy(z4_bottom, m_s.at[pl.ds(9 * rows + half, half)], m_sem.at[10])
    )
    depth = w_s.shape[0] // (2 * NX)
    copies_w = []
    for who in range(2):
        for i, distance in enumerate((0, -1, 1, 2, 2)):
            piece = pieces[who * 5 + i]
            from_x = lax.rem(x + distance + NX, NX)
            from_core = core if who == 0 else 1 - core
            start = (2 * from_x + from_core) * depth
            if i == 4:
                start = start + depth // 2
            start = pl.multiple_of(start, 16)
            copies_w.append(
                pltpu.make_async_copy(
                    piece, w_s.at[pl.ds(start, piece.shape[0])], w_sem.at[who * 5 + i]
                )
            )
    copies_m[0].start()
    for copy in copies_w:
        copy.start()
    for copy in copies_m[1:]:
        copy.start()

    low = lax.rem(frame, NY) < 2
    two_a = jnp.where(low, 2, -2)
    offsets = (0, -4, 4, two_a, -8, 8, -1, 1, -two_a)
    for i in range(N_SLABS):
        if i < 9:
            source = frame + offsets[i]
        else:
            source = lax.rem(frame + 16, 32)
        inside = jnp.logical_and(source >= 0, source < 32)
        source = jnp.clip(source, 0, 31)
        for q_block in range(2):
            for k_block in range(2):
                ok = jnp.logical_and(inside, mask_ref[q_block, 2 * source + k_block] > 0)
                bias_s[q_block : q_block + 1, pl.ds(i * rows + k_block * BLK, BLK)] = jnp.full(
                    (1, BLK), jnp.where(ok, 0.0, -jnp.inf), F32
                )

    def rms(value, gain):
        square = jnp.mean(value * value, axis=-1, keepdims=True)
        return (value * lax.rsqrt(square + NORM_EPS) * gain).astype(BF16)

    copies_m[0].wait()
    for copy in copies_w:
        copy.wait()
    projected = jnp.dot(m_s[0:rows], w_s[:, 0:feats], preferred_element_type=F32)
    q_s[...] = rms(projected, gain_ref[0:1, :])
    for copy in copies_m[1:]:
        copy.wait()

    span = 2 * rows

    def project(i, carry):
        at = pl.ds(pl.multiple_of(i * span, span), span)
        block = m_s[at]
        keys = jnp.dot(block, w_s[:, feats : 2 * feats], preferred_element_type=F32)
        k_s[at] = rms(keys, gain_ref[1:2, :])
        values = jnp.dot(block, w_s[:, 2 * feats :], preferred_element_type=F32)
        v_s[at] = values.astype(BF16)
        return carry

    lax.fori_loop(0, N_SLABS // 2, project, 0)

    factor = 1.0 / math.sqrt(HD)
    for head in range(feats // HD):
        cols = slice(head * HD, (head + 1) * HD)
        for q_block in range(rows // BLK):
            at = slice(q_block * BLK, (q_block + 1) * BLK)
            scores = lax.dot_general(
                q_s[at, cols], k_s[:, cols], (((1,), (1,)), ((), ())), preferred_element_type=F32
            )
            scores = scores * factor + bias_s[q_block : q_block + 1, :]
            peak = jnp.max(scores, axis=-1, keepdims=True)
            terms = jnp.exp(scores - peak)
            total = jnp.sum(terms, axis=-1, keepdims=True)
            mixed = jnp.dot(terms.astype(BF16), v_s[:, cols], preferred_element_type=F32)
            out_ref[at, cols] = (mixed / total).astype(BF16)


def attend(where, block_mask, norm_gain, slabs, pieces):
    rows, width = slabs[0].shape
    feats = norm_gain.shape[1]
    keys = N_SLABS * rows
    any_spec = pl.BlockSpec(memory_space=pl.ANY)
    smem = pl.BlockSpec(memory_space=pltpu.SMEM)
    return pl.pallas_call(
        attend_kernel,
        in_specs=[smem, smem, pl.BlockSpec(memory_space=pltpu.VMEM)]
        + [any_spec] * (len(slabs) + len(pieces)),
        out_specs=pl.BlockSpec(memory_space=pltpu.VMEM),
        out_shape=jax.ShapeDtypeStruct((rows, feats), BF16),
        scratch_shapes=[
            pltpu.VMEM((keys, width), BF16),
            pltpu.VMEM((width, 3 * feats), BF16),
            pltpu.VMEM((keys, feats), BF16),
            pltpu.VMEM((keys, feats), BF16),
            pltpu.VMEM((rows, feats), BF16),
            pltpu.VMEM((2, keys), F32),
            pltpu.SemaphoreType.DMA((11,)),
            pltpu.SemaphoreType.DMA((10,)),
        ],
        compiler_params=pltpu.CompilerParams(vmem_limit_bytes=VMEM_LIMIT),
        cost_estimate=pl.CostEstimate(
            flops=16_000_000_000, bytes_accessed=16_000_000, transcendentals=4_000_000
        ),
        name="attend",
    )(where, block_mask, norm_gain, *slabs, *pieces)


def output_kernel(where_ref, index_ref, mixed_ref, row_ref, *refs):
    pieces = refs[:8]
    out_ref, w_s, sem = refs[8:]
    x, core = where_ref[1], where_ref[2]
    depth = w_s.shape[0] // (2 * NX)
    copies = []
    for who in range(2):
        for i, distance in enumerate((0, -1, 1, 2)):
            from_x = lax.rem(x + distance + NX, NX)
            from_core = core if who == 0 else 1 - core
            start = pl.multiple_of((2 * from_x + from_core) * depth, 16)
            copies.append(
                pltpu.make_async_copy(
                    pieces[who * 4 + i], w_s.at[pl.ds(start, depth)], sem.at[who * 4 + i]
                )
            )
    for copy in copies:
        copy.start()
    for copy in copies:
        copy.wait()
    rows = jnp.dot(mixed_ref[...], w_s[...], preferred_element_type=F32)
    out_ref[...] = (row_ref[0, 2:3, :] * rows).astype(BF16)


def output(where, step_index, mixed, modulation, pieces):
    rows, feats = mixed.shape
    width = modulation.shape[2]
    any_spec = pl.BlockSpec(memory_space=pl.ANY)
    return pl.pallas_call(
        output_kernel,
        grid_spec=pltpu.PrefetchScalarGridSpec(
            num_scalar_prefetch=2,
            grid=(1,),
            in_specs=[
                pl.BlockSpec((rows, feats), lambda i, w, s: (0, 0)),
                pl.BlockSpec((1, 3, width), lambda i, w, s: (s[w[0]], 0, 0)),
            ]
            + [any_spec] * 8,
            out_specs=pl.BlockSpec((rows, width), lambda i, w, s: (0, 0)),
            scratch_shapes=[
                pltpu.VMEM((feats, width), BF16),
                pltpu.SemaphoreType.DMA((8,)),
            ],
        ),
        out_shape=jax.ShapeDtypeStruct((rows, width), BF16),
        compiler_params=pltpu.CompilerParams(vmem_limit_bytes=VMEM_LIMIT),
        name="output",
    )(where, step_index, mixed, modulation, *pieces)


def rolled(parts, own):
    count = len(parts)
    doubled = jnp.stack(parts + parts)
    return lax.dynamic_slice_in_dim(doubled, lax.rem(count - own, count), count, 0)


def on_device(
    latents,
    anchor,
    step_index,
    modulation,
    step_sizes,
    input_weight,
    output_weight,
    norm_gain,
    block_mask,
):
    latent = latents[0]
    rows, width = latent.shape
    step = lax.axis_index("step")
    frame = lax.axis_index("frame")
    x, core = step // 2, lax.rem(step, 2)
    z, y = frame // NY, lax.rem(frame, NY)
    where_am_i = jnp.stack([step, x, core, frame]).astype(jnp.int32)

    out_width = output_weight.shape[1]
    packed = jnp.concatenate([input_weight, output_weight.reshape(2, -1)], axis=0)
    parts = [packed, y_shift(packed, -1), y_shift(packed, 2), y_shift(packed, 1)]
    column = rolled(parts, y)
    column = jnp.concatenate(
        [column[:, :6].reshape(24, -1), column[:, 6:].reshape(8, -1)], axis=0
    )

    modulated = modulate(where_am_i, step_index, latent, modulation)

    up1, down1 = z_shift(column, 1), z_shift(column, -1)
    up2, down2 = z_shift(up1, 1), z_shift(down1, -1)
    up3, down3 = z_shift(up2, 1), z_shift(down2, -1)
    up4 = z_shift(up3, 1)
    plane = rolled([column, down1, down2, down3, up4, up3, up2, up1], z)
    in_rows = plane[:, :24].reshape(192, -1)
    out_rows = plane[:, 24:].reshape(96, out_width)

    zp, zm = z_shift(modulated, 1), z_shift(modulated, -1)
    two_a = y_shift(modulated, 2)
    zp2, zm2 = z_shift(zp, 1), z_shift(zm, -1)
    before = y_shift(jnp.where(y == NY - 1, zp, modulated), 1)
    after = y_shift(jnp.where(y == 0, zm, modulated), -1)
    z4_top = z_shift(zp2[: rows // 2], 2)
    z4_bottom = z_shift(zm2[rows // 2 :], -2)
    two_b = y_shift(jnp.where(y >= 2, zp, zm), 2)
    slabs = [modulated, zp, zm, two_a, zp2, zm2, before, after, two_b, z4_top, z4_bottom]

    left, right = x_shift(in_rows, 1), x_shift(in_rows, -1)
    far_top = x_shift(left[:96], 1)
    far_bottom = x_shift(right[96:], -1)
    pieces = [in_rows, left, right, far_top, far_bottom]
    pieces = pieces + [core_swap(piece) for piece in pieces]
    mixed = attend(where_am_i, block_mask, norm_gain, slabs, pieces)

    out_pieces = [out_rows, x_shift(out_rows, 1), x_shift(out_rows, -1), x_shift(out_rows, 2)]
    out_pieces = out_pieces + [core_swap(piece) for piece in out_pieces]
    velocity = output(where_am_i, step_index, mixed, modulation, out_pieces)

    size_own = step_sizes[step_index[step]]
    size_other = step_sizes[step_index[step ^ 1]]
    half = rows // 2
    other = core_swap(velocity)
    own_half = lax.dynamic_slice_in_dim(velocity, core * half, half, 0).astype(F32)
    other_half = lax.dynamic_slice_in_dim(other, core * half, half, 0).astype(F32)
    chip_total = (size_own * own_half + size_other * other_half).astype(BF16)
    one = x_later(chip_total, 1)
    two = x_later(one, 1)
    three = x_later(chip_total, 3)
    earlier = (one.astype(F32) + two.astype(F32) + three.astype(F32)).astype(BF16)
    swapped = core_swap(earlier)
    first = jnp.where(core == 0, earlier, swapped)
    second = jnp.where(core == 0, swapped, earlier)
    prefix = jnp.concatenate([first, second], axis=0).astype(F32)
    inner = jnp.where(core == 1, size_other, 0.0)
    advanced = (
        anchor + prefix + inner * other.astype(F32) + size_own * velocity.astype(F32)
    )
    return (velocity[None], advanced[None])


def solution(mesh):
    placed = (
        P("step", "frame", None),
        P("frame", None),
        P(),
        P(),
        P(),
        P(("step", "frame"), None),
        P(("step", "frame"), None),
        P(),
        P("frame", None),
    )
    return jax.shard_map(
        on_device,
        mesh=mesh,
        in_specs=placed,
        out_specs=(P("step", "frame", None), P("step", "frame", None)),
        check_vma=False,
    )
```

```python
import functools
import math

import jax
import jax.numpy as jnp
from jax import lax
from jax.experimental import pallas as pl
from jax.experimental.pallas import tpu as pltpu
from jax.sharding import PartitionSpec as P

HD = 128
BLK = 128
NX, NY, NZ = 4, 4, 8
NORM_EPS = 1e-06
F32 = jnp.float32
BF16 = jnp.bfloat16
VMEM_LIMIT = 56 * 1024 * 1024


def y_shift(block, distance):
    pairs = [(4 * z + y, 4 * z + (y + distance) % NY) for z in range(NZ) for y in range(NY)]
    return lax.ppermute(block, "frame", pairs)


def z_shift(block, distance):
    pairs = [(4 * z + y, 4 * ((z + distance) % NZ) + y) for z in range(NZ) for y in range(NY)]
    return lax.ppermute(block, "frame", pairs)


def x_shift(block, distance):
    pairs = [(2 * x + c, 2 * ((x + distance) % NX) + c) for x in range(NX) for c in range(2)]
    return lax.ppermute(block, "step", pairs)


def x_later(block, distance):
    pairs = [(2 * x + c, 2 * (x + distance) + c) for x in range(NX - distance) for c in range(2)]
    return lax.ppermute(block, "step", pairs)


def core_swap(block):
    return lax.ppermute(block, "step", [(i, i ^ 1) for i in range(2 * NX)])


def modulate_kernel(where_ref, index_ref, latent_ref, table_ref, out_ref, row_s, sem):
    own = index_ref[where_ref[0]]
    copies = [
        pltpu.make_async_copy(table_ref.at[i, pl.ds(own, 1)], row_s.at[i], sem.at[i])
        for i in range(2)
    ]
    for copy in copies:
        copy.start()
    value = latent_ref[...].astype(F32)
    centered = value - jnp.mean(value, axis=-1, keepdims=True)
    variance = jnp.mean(centered * centered, axis=-1, keepdims=True)
    normed = centered * lax.rsqrt(variance + NORM_EPS)
    for copy in copies:
        copy.wait()
    out_ref[...] = (normed * (1.0 + row_s[1]) + row_s[0]).astype(BF16)


def modulate(where, step_index, latent, table):
    rows, width = latent.shape
    return pl.pallas_call(
        modulate_kernel,
        in_specs=[
            pl.BlockSpec(memory_space=pltpu.SMEM),
            pl.BlockSpec(memory_space=pltpu.SMEM),
            pl.BlockSpec(memory_space=pltpu.VMEM),
            pl.BlockSpec(memory_space=pl.ANY),
        ],
        out_specs=pl.BlockSpec(memory_space=pltpu.VMEM),
        out_shape=jax.ShapeDtypeStruct((rows, width), BF16),
        scratch_shapes=[pltpu.VMEM((2, 1, width), F32), pltpu.SemaphoreType.DMA((2,))],
        name="modulate",
    )(where, step_index, latent, table)


N_SLABS = 10


def attend_kernel(
    where_ref,
    mask_ref,
    gain_ref,
    *refs,
):
    slabs = refs[:9]
    z4_top, z4_bottom = refs[9:11]
    pieces = refs[11:21]
    keep_ref, send_ref = refs[21:23]
    m_s, w_s, k_s, v_s, q_s, bias_s, m_sem, w_sem = refs[23:]
    x, core, frame = where_ref[1], where_ref[2], where_ref[3]
    rows = q_s.shape[0]
    feats = q_s.shape[1]
    half = rows // 2

    copies_m = []
    for i in range(9):
        copies_m.append(pltpu.make_async_copy(slabs[i], m_s.at[pl.ds(i * rows, rows)], m_sem.at[i]))
    copies_m.append(pltpu.make_async_copy(z4_top, m_s.at[pl.ds(9 * rows, half)], m_sem.at[9]))
    copies_m.append(
        pltpu.make_async_copy(z4_bottom, m_s.at[pl.ds(9 * rows + half, half)], m_sem.at[10])
    )
    depth = w_s.shape[0] // (2 * NX)
    copies_w = []
    for who in range(2):
        for i, distance in enumerate((0, -1, 1, 2, 2)):
            piece = pieces[who * 5 + i]
            from_x = lax.rem(x + distance + NX, NX)
            from_core = core if who == 0 else 1 - core
            start = (2 * from_x + from_core) * depth
            if i == 4:
                start = start + depth // 2
            start = pl.multiple_of(start, 16)
            copies_w.append(
                pltpu.make_async_copy(
                    piece, w_s.at[pl.ds(start, piece.shape[0])], w_sem.at[who * 5 + i]
                )
            )
    copies_m[0].start()
    for copy in copies_w:
        copy.start()
    for copy in copies_m[1:]:
        copy.start()

    low = lax.rem(frame, NY) < 2
    two_a = jnp.where(low, 2, -2)
    offsets = (0, -4, 4, two_a, -8, 8, -1, 1, -two_a)
    for i in range(N_SLABS):
        if i < 9:
            source = frame + offsets[i]
        else:
            source = lax.rem(frame + 16, 32)
        inside = jnp.logical_and(source >= 0, source < 32)
        source = jnp.clip(source, 0, 31)
        for q_block in range(2):
            for k_block in range(2):
                ok = jnp.logical_and(inside, mask_ref[q_block, 2 * source + k_block] > 0)
                bias_s[q_block : q_block + 1, pl.ds(i * rows + k_block * BLK, BLK)] = jnp.full(
                    (1, BLK), jnp.where(ok, 0.0, -jnp.inf), F32
                )

    def rms(value, gain):
        square = jnp.mean(value * value, axis=-1, keepdims=True)
        return (value * lax.rsqrt(square + NORM_EPS) * gain).astype(BF16)

    copies_m[0].wait()
    for copy in copies_w:
        copy.wait()
    projected = jnp.dot(m_s[0:rows], w_s[:, 0:feats], preferred_element_type=F32)
    q_s[...] = rms(projected, gain_ref[0:1, :])
    for copy in copies_m[1:]:
        copy.wait()

    span = 2 * rows

    def project(i, carry):
        at = pl.ds(pl.multiple_of(i * span, span), span)
        block = m_s[at]
        keys = jnp.dot(block, w_s[:, feats : 2 * feats], preferred_element_type=F32)
        k_s[at] = rms(keys, gain_ref[1:2, :])
        values = jnp.dot(block, w_s[:, 2 * feats :], preferred_element_type=F32)
        v_s[at] = values.astype(BF16)
        return carry

    lax.fori_loop(0, N_SLABS // 2, project, 0)

    factor = 1.0 / math.sqrt(HD)
    for out_ref, q_block in ((send_ref, 1 - core), (keep_ref, core)):
        at = pl.ds(pl.multiple_of(q_block * BLK, BLK), BLK)
        bias = bias_s[pl.ds(q_block, 1), :]
        for head in range(feats // HD):
            cols = slice(head * HD, (head + 1) * HD)
            scores = lax.dot_general(
                q_s[at, cols], k_s[:, cols], (((1,), (1,)), ((), ())), preferred_element_type=F32
            )
            scores = scores * factor + bias
            peak = jnp.max(scores, axis=-1, keepdims=True)
            terms = jnp.exp(scores - peak)
            total = jnp.sum(terms, axis=-1, keepdims=True)
            mixed = jnp.dot(terms.astype(BF16), v_s[:, cols], preferred_element_type=F32)
            out_ref[:, cols] = (mixed / total).astype(BF16)


def attend(where, block_mask, norm_gain, slabs, pieces):
    rows, width = slabs[0].shape
    feats = norm_gain.shape[1]
    keys = N_SLABS * rows
    any_spec = pl.BlockSpec(memory_space=pl.ANY)
    smem = pl.BlockSpec(memory_space=pltpu.SMEM)
    return pl.pallas_call(
        attend_kernel,
        in_specs=[smem, smem, pl.BlockSpec(memory_space=pltpu.VMEM)]
        + [any_spec] * (len(slabs) + len(pieces)),
        out_specs=[pl.BlockSpec(memory_space=pltpu.VMEM)] * 2,
        out_shape=[jax.ShapeDtypeStruct((BLK, feats), BF16)] * 2,
        scratch_shapes=[
            pltpu.VMEM((keys, width), BF16),
            pltpu.VMEM((width, 3 * feats), BF16),
            pltpu.VMEM((keys, feats), BF16),
            pltpu.VMEM((keys, feats), BF16),
            pltpu.VMEM((rows, feats), BF16),
            pltpu.VMEM((2, keys), F32),
            pltpu.SemaphoreType.DMA((11,)),
            pltpu.SemaphoreType.DMA((10,)),
        ],
        compiler_params=pltpu.CompilerParams(vmem_limit_bytes=VMEM_LIMIT),
        cost_estimate=pl.CostEstimate(
            flops=16_000_000_000, bytes_accessed=16_000_000, transcendentals=4_000_000
        ),
        name="attend",
    )(where, block_mask, norm_gain, *slabs, *pieces)


def output_kernel(where_ref, index_ref, size_ref, keep_ref, got_ref, table_ref, *refs):
    pieces = refs[:8]
    own_ref, other_ref, total_ref, w_s, row_s, sem, row_sem = refs[8:]
    step, x, core = where_ref[0], where_ref[1], where_ref[2]
    own_index = index_ref[step]
    other_index = index_ref[step + 1 - 2 * core]
    depth = w_s.shape[0] // (2 * NX)
    copies = []
    for who in range(2):
        for i, distance in enumerate((0, -1, 1, 2)):
            from_x = lax.rem(x + distance + NX, NX)
            from_core = core if who == 0 else 1 - core
            start = pl.multiple_of((2 * from_x + from_core) * depth, 16)
            copies.append(
                pltpu.make_async_copy(
                    pieces[who * 4 + i], w_s.at[pl.ds(start, depth)], sem.at[who * 4 + i]
                )
            )
    for i, index in enumerate((own_index, other_index)):
        copies.append(
            pltpu.make_async_copy(table_ref.at[2, pl.ds(index, 1)], row_s.at[i], row_sem.at[i])
        )
    for copy in copies:
        copy.start()
    for copy in copies:
        copy.wait()
    weight = w_s[...]
    own = jnp.dot(keep_ref[...], weight, preferred_element_type=F32)
    own = (row_s[0] * own).astype(BF16)
    other = jnp.dot(got_ref[...], weight, preferred_element_type=F32)
    other = (row_s[1] * other).astype(BF16)
    own_ref[...] = own
    other_ref[...] = other
    total_ref[...] = (
        size_ref[own_index] * own.astype(F32) + size_ref[other_index] * other.astype(F32)
    ).astype(BF16)


def output(where, step_index, step_sizes, keep, got, table, pieces):
    half, feats = keep.shape
    width = table.shape[2]
    any_spec = pl.BlockSpec(memory_space=pl.ANY)
    vmem = pl.BlockSpec(memory_space=pltpu.VMEM)
    smem = pl.BlockSpec(memory_space=pltpu.SMEM)
    return pl.pallas_call(
        output_kernel,
        in_specs=[smem, smem, smem, vmem, vmem] + [any_spec] * 9,
        out_specs=[vmem] * 3,
        scratch_shapes=[
            pltpu.VMEM((feats, width), BF16),
            pltpu.VMEM((2, 1, width), F32),
            pltpu.SemaphoreType.DMA((8,)),
            pltpu.SemaphoreType.DMA((2,)),
        ],
        out_shape=[jax.ShapeDtypeStruct((half, width), BF16)] * 3,
        compiler_params=pltpu.CompilerParams(vmem_limit_bytes=VMEM_LIMIT),
        name="output",
    )(where, step_index, step_sizes, keep, got, table, *pieces)


def earlier_kernel(where_ref, index_ref, size_ref, one_ref, two_ref, three_ref, own_ref, out_ref):
    core = where_ref[2]
    size = jnp.where(core == 0, size_ref[index_ref[where_ref[0]]], 0.0)
    total = one_ref[...].astype(F32) + two_ref[...].astype(F32) + three_ref[...].astype(F32)
    out_ref[...] = (total + size * own_ref[...].astype(F32)).astype(BF16)


def earlier_sum(where, step_index, step_sizes, one, two, three, own):
    vmem = pl.BlockSpec(memory_space=pltpu.VMEM)
    smem = pl.BlockSpec(memory_space=pltpu.SMEM)
    return pl.pallas_call(
        earlier_kernel,
        in_specs=[smem, smem, smem] + [vmem] * 4,
        out_specs=vmem,
        out_shape=jax.ShapeDtypeStruct(own.shape, BF16),
        name="earlier_sum",
    )(where, step_index, step_sizes, one, two, three, own)


def advance_kernel(
    where_ref,
    index_ref,
    size_ref,
    one_ref,
    two_ref,
    three_ref,
    own_ref,
    other_ref,
    before_ref,
    rest_ref,
    anchor_ref,
    velocity_ref,
    advanced_ref,
):
    step, core = where_ref[0], where_ref[2]
    half = own_ref.shape[0]
    size_own = size_ref[index_ref[step]]
    size_other = jnp.where(core == 1, size_ref[index_ref[step + 1 - 2 * core]], 0.0)
    near = pl.ds(pl.multiple_of(core * half, half), half)
    far = pl.ds(pl.multiple_of((1 - core) * half, half), half)
    own = own_ref[...]
    velocity_ref[near] = own
    total = one_ref[...].astype(F32) + two_ref[...].astype(F32) + three_ref[...].astype(F32)
    total = total + size_other * other_ref[...].astype(F32) + size_own * own.astype(F32)
    advanced_ref[near] = anchor_ref[near] + total
    rest = rest_ref[...]
    velocity_ref[far] = rest
    advanced_ref[far] = (
        anchor_ref[far] + before_ref[...].astype(F32) + size_own * rest.astype(F32)
    )


def advance(where, step_index, step_sizes, one, two, three, own, other, before, rest, anchor):
    vmem = pl.BlockSpec(memory_space=pltpu.VMEM)
    smem = pl.BlockSpec(memory_space=pltpu.SMEM)
    return pl.pallas_call(
        advance_kernel,
        in_specs=[smem, smem, smem] + [vmem] * 8,
        out_specs=[vmem] * 2,
        out_shape=[
            jax.ShapeDtypeStruct(anchor.shape, BF16),
            jax.ShapeDtypeStruct(anchor.shape, F32),
        ],
        name="advance",
    )(where, step_index, step_sizes, one, two, three, own, other, before, rest, anchor)


def placed_z(parts, own):
    result = jnp.zeros((len(parts),) + parts[0].shape, BF16)
    for i, part in enumerate(parts):
        result = lax.dynamic_update_slice_in_dim(result, part[None], lax.rem(own + i, NZ), 0)
    return result


def placed_y(parts, own):
    result = jnp.zeros((NZ, NY, 8, parts[0].shape[1]), BF16)
    for i, part in enumerate(parts):
        part = part.reshape(NZ, 1, 8, -1)
        result = lax.dynamic_update_slice_in_dim(result, part, lax.rem(own + i, NY), 1)
    return result


def on_device(
    latents,
    anchor,
    step_index,
    modulation,
    step_sizes,
    input_weight,
    output_weight,
    norm_gain,
    block_mask,
):
    latent = latents[0]
    rows, width = latent.shape
    step = lax.axis_index("step")
    frame = lax.axis_index("frame")
    x, core = step // 2, lax.rem(step, 2)
    z, y = frame // NY, lax.rem(frame, NY)
    where_am_i = jnp.stack([step, x, core, frame]).astype(jnp.int32)

    table = jnp.transpose(modulation, (1, 0, 2))

    out_width = output_weight.shape[1]
    packed = jnp.concatenate([input_weight, output_weight.reshape(2, -1)], axis=0)
    parts = [packed] + [z_shift(packed, -d) for d in range(1, NZ)]
    modulated = modulate(where_am_i, step_index, latent, table)
    column = placed_z(parts, z).reshape(8 * NZ, -1)
    column, modulated = lax.optimization_barrier((column, modulated))
    plane = placed_y([column] + [y_shift(column, -d) for d in range(1, NY)], y)
    in_rows = plane[:, :, :6].reshape(192, -1)
    out_rows = plane[:, :, 6:].reshape(96, out_width)

    zp, zm = z_shift(modulated, 1), z_shift(modulated, -1)
    two_a = y_shift(lax.optimization_barrier((modulated, plane))[0], 2)
    zp2, zm2 = z_shift(zp, 1), z_shift(zm, -1)
    before = y_shift(jnp.where(y == NY - 1, zp, modulated), 1)
    after = y_shift(jnp.where(y == 0, zm, modulated), -1)
    z4_top = z_shift(zp2[: rows // 2], 2)
    z4_bottom = z_shift(zm2[rows // 2 :], -2)
    two_b = y_shift(jnp.where(y >= 2, zp, zm), 2)
    slabs = [modulated, zp, zm, two_a, zp2, zm2, before, after, two_b, z4_top, z4_bottom]

    left, right = x_shift(in_rows, 1), x_shift(in_rows, -1)
    far_top = x_shift(left[:96], 1)
    far_bottom = x_shift(right[96:], -1)
    pieces = [in_rows, left, right, far_top, far_bottom]
    pieces = pieces + [core_swap(piece) for piece in pieces]
    out_pieces = [out_rows, x_shift(out_rows, 1), x_shift(out_rows, -1), x_shift(out_rows, 2)]
    out_pieces = out_pieces + [core_swap(piece) for piece in out_pieces]
    keep, send = attend(where_am_i, block_mask, norm_gain, slabs, pieces)

    got = core_swap(send)
    own, other, total = output(
        where_am_i, step_index, step_sizes, keep, got, table, out_pieces
    )
    one = x_later(total, 1)
    three = x_later(total, 3)
    two = x_later(one, 1)
    rest = core_swap(other)
    sums = earlier_sum(where_am_i, step_index, step_sizes, one, two, three, own)
    before = core_swap(sums)
    velocity, advanced = advance(
        where_am_i, step_index, step_sizes, one, two, three, own, other, before, rest, anchor
    )
    return (velocity[None], advanced[None])


def solution(mesh):
    placed = (
        P("step", "frame", None),
        P("frame", None),
        P(),
        P(),
        P(),
        P(("step", "frame"), None),
        P(("step", "frame"), None),
        P(),
        P("frame", None),
    )
    return jax.shard_map(
        on_device,
        mesh=mesh,
        in_specs=placed,
        out_specs=(P("step", "frame", None), P("step", "frame", None)),
        check_vma=False,
    )
```

```python
import functools
import math

import jax
import jax.numpy as jnp
from jax import lax
from jax.experimental import pallas as pl
from jax.experimental.pallas import tpu as pltpu
from jax.sharding import PartitionSpec as P

HD = 128
BLK = 128
NX, NY, NZ = 4, 4, 8
NORM_EPS = 1e-06
F32 = jnp.float32
BF16 = jnp.bfloat16
VMEM_LIMIT = 56 * 1024 * 1024


def y_shift(block, distance):
    pairs = [(4 * z + y, 4 * z + (y + distance) % NY) for z in range(NZ) for y in range(NY)]
    return lax.ppermute(block, "frame", pairs)


def z_shift(block, distance):
    pairs = [(4 * z + y, 4 * ((z + distance) % NZ) + y) for z in range(NZ) for y in range(NY)]
    return lax.ppermute(block, "frame", pairs)


def x_shift(block, distance):
    pairs = [(2 * x + c, 2 * ((x + distance) % NX) + c) for x in range(NX) for c in range(2)]
    return lax.ppermute(block, "step", pairs)


def x_later(block, distance):
    pairs = [(2 * x + c, 2 * (x + distance) + c) for x in range(NX - distance) for c in range(2)]
    return lax.ppermute(block, "step", pairs)


def core_swap(block):
    return lax.ppermute(block, "step", [(i, i ^ 1) for i in range(2 * NX)])


def modulate_kernel(where_ref, index_ref, latent_ref, table_ref, out_ref, row_s, sem):
    own = index_ref[where_ref[0]]
    copies = [
        pltpu.make_async_copy(table_ref.at[i, pl.ds(own, 1)], row_s.at[i], sem.at[i])
        for i in range(2)
    ]
    for copy in copies:
        copy.start()
    value = latent_ref[...].astype(F32)
    centered = value - jnp.mean(value, axis=-1, keepdims=True)
    variance = jnp.mean(centered * centered, axis=-1, keepdims=True)
    normed = centered * lax.rsqrt(variance + NORM_EPS)
    for copy in copies:
        copy.wait()
    out_ref[...] = (normed * (1.0 + row_s[1]) + row_s[0]).astype(BF16)


def modulate(where, step_index, latent, table):
    rows, width = latent.shape
    return pl.pallas_call(
        modulate_kernel,
        in_specs=[
            pl.BlockSpec(memory_space=pltpu.SMEM),
            pl.BlockSpec(memory_space=pltpu.SMEM),
            pl.BlockSpec(memory_space=pltpu.VMEM),
            pl.BlockSpec(memory_space=pl.ANY),
        ],
        out_specs=pl.BlockSpec(memory_space=pltpu.VMEM),
        out_shape=jax.ShapeDtypeStruct((rows, width), BF16),
        scratch_shapes=[pltpu.VMEM((2, 1, width), F32), pltpu.SemaphoreType.DMA((2,))],
        name="modulate",
    )(where, step_index, latent, table)


N_SLABS = 10


def attend_kernel(
    where_ref,
    mask_ref,
    gain_ref,
    *refs,
):
    slabs = refs[:9]
    z4_top, z4_bottom = refs[9:11]
    pieces = refs[11:21]
    keep_ref, send_ref = refs[21:23]
    m_s, w_s, k_s, v_s, q_s, bias_s, m_sem, w_sem = refs[23:]
    x, core, frame = where_ref[1], where_ref[2], where_ref[3]
    rows = q_s.shape[0]
    feats = q_s.shape[1]
    half = rows // 2

    copies_m = []
    for i in range(9):
        copies_m.append(pltpu.make_async_copy(slabs[i], m_s.at[pl.ds(i * rows, rows)], m_sem.at[i]))
    copies_m.append(pltpu.make_async_copy(z4_top, m_s.at[pl.ds(9 * rows, half)], m_sem.at[9]))
    copies_m.append(
        pltpu.make_async_copy(z4_bottom, m_s.at[pl.ds(9 * rows + half, half)], m_sem.at[10])
    )
    depth = w_s.shape[0] // (2 * NX)
    copies_w = []
    for who in range(2):
        for i, distance in enumerate((0, -1, 1, 2, 2)):
            piece = pieces[who * 5 + i]
            from_x = lax.rem(x + distance + NX, NX)
            from_core = core if who == 0 else 1 - core
            start = (2 * from_x + from_core) * depth
            if i == 4:
                start = start + depth // 2
            start = pl.multiple_of(start, 16)
            copies_w.append(
                pltpu.make_async_copy(
                    piece, w_s.at[pl.ds(start, piece.shape[0])], w_sem.at[who * 5 + i]
                )
            )
    copies_m[0].start()
    for copy in copies_w:
        copy.start()
    for copy in copies_m[1:]:
        copy.start()

    low = lax.rem(frame, NY) < 2
    two_a = jnp.where(low, 2, -2)
    offsets = (0, -4, 4, two_a, -8, 8, -1, 1, -two_a)
    for i in range(N_SLABS):
        if i < 9:
            source = frame + offsets[i]
        else:
            source = lax.rem(frame + 16, 32)
        inside = jnp.logical_and(source >= 0, source < 32)
        source = jnp.clip(source, 0, 31)
        for q_block in range(2):
            for k_block in range(2):
                ok = jnp.logical_and(inside, mask_ref[q_block, 2 * source + k_block] > 0)
                bias_s[q_block : q_block + 1, pl.ds(i * rows + k_block * BLK, BLK)] = jnp.full(
                    (1, BLK), jnp.where(ok, 0.0, -jnp.inf), F32
                )

    def rms(value, gain):
        square = jnp.mean(value * value, axis=-1, keepdims=True)
        return (value * lax.rsqrt(square + NORM_EPS) * gain).astype(BF16)

    copies_m[0].wait()
    for copy in copies_w:
        copy.wait()
    projected = jnp.dot(m_s[0:rows], w_s[:, 0:feats], preferred_element_type=F32)
    q_s[...] = rms(projected, gain_ref[0:1, :])
    for copy in copies_m[1:]:
        copy.wait()

    span = 2 * rows

    def project(i, carry):
        at = pl.ds(pl.multiple_of(i * span, span), span)
        block = m_s[at]
        keys = jnp.dot(block, w_s[:, feats : 2 * feats], preferred_element_type=F32)
        k_s[at] = rms(keys, gain_ref[1:2, :])
        values = jnp.dot(block, w_s[:, 2 * feats :], preferred_element_type=F32)
        v_s[at] = values.astype(BF16)
        return carry

    lax.fori_loop(0, N_SLABS // 2, project, 0)

    factor = 1.0 / math.sqrt(HD)
    for out_ref, q_block in ((send_ref, 1 - core), (keep_ref, core)):
        at = pl.ds(pl.multiple_of(q_block * BLK, BLK), BLK)
        bias = bias_s[pl.ds(q_block, 1), :]
        for head in range(feats // HD):
            cols = slice(head * HD, (head + 1) * HD)
            scores = lax.dot_general(
                q_s[at, cols], k_s[:, cols], (((1,), (1,)), ((), ())), preferred_element_type=F32
            )
            scores = scores * factor + bias
            peak = jnp.max(scores, axis=-1, keepdims=True)
            terms = jnp.exp(scores - peak)
            total = jnp.sum(terms, axis=-1, keepdims=True)
            mixed = jnp.dot(terms.astype(BF16), v_s[:, cols], preferred_element_type=F32)
            out_ref[:, cols] = (mixed / total).astype(BF16)


def attend(where, block_mask, norm_gain, slabs, pieces):
    rows, width = slabs[0].shape
    feats = norm_gain.shape[1]
    keys = N_SLABS * rows
    any_spec = pl.BlockSpec(memory_space=pl.ANY)
    smem = pl.BlockSpec(memory_space=pltpu.SMEM)
    return pl.pallas_call(
        attend_kernel,
        in_specs=[smem, smem, pl.BlockSpec(memory_space=pltpu.VMEM)]
        + [any_spec] * (len(slabs) + len(pieces)),
        out_specs=[pl.BlockSpec(memory_space=pltpu.VMEM)] * 2,
        out_shape=[jax.ShapeDtypeStruct((BLK, feats), BF16)] * 2,
        scratch_shapes=[
            pltpu.VMEM((keys, width), BF16),
            pltpu.VMEM((width, 3 * feats), BF16),
            pltpu.VMEM((keys, feats), BF16),
            pltpu.VMEM((keys, feats), BF16),
            pltpu.VMEM((rows, feats), BF16),
            pltpu.VMEM((2, keys), F32),
            pltpu.SemaphoreType.DMA((11,)),
            pltpu.SemaphoreType.DMA((10,)),
        ],
        compiler_params=pltpu.CompilerParams(vmem_limit_bytes=VMEM_LIMIT),
        cost_estimate=pl.CostEstimate(
            flops=16_000_000_000, bytes_accessed=16_000_000, transcendentals=4_000_000
        ),
        name="attend",
    )(where, block_mask, norm_gain, *slabs, *pieces)


def output_kernel(where_ref, index_ref, size_ref, keep_ref, got_ref, table_ref, *refs):
    pieces = refs[:4]
    own_ref, other_ref, total_ref, w_s, row_s, sem, row_sem = refs[4:]
    step, x, core = where_ref[0], where_ref[1], where_ref[2]
    own_index = index_ref[step]
    other_index = index_ref[step + 1 - 2 * core]
    depth = w_s.shape[0] // (2 * NX)
    copies = []
    for who in range(2):
        for i, distance in enumerate((0, -1, 1, 2)):
            from_x = lax.rem(x + distance + NX, NX)
            from_core = core if who == 0 else 1 - core
            start = pl.multiple_of((2 * from_x + from_core) * depth, 16)
            copies.append(
                pltpu.make_async_copy(
                    pieces[i].at[who], w_s.at[pl.ds(start, depth)], sem.at[who * 4 + i]
                )
            )
    for i, index in enumerate((own_index, other_index)):
        copies.append(
            pltpu.make_async_copy(table_ref.at[2, pl.ds(index, 1)], row_s.at[i], row_sem.at[i])
        )
    for copy in copies:
        copy.start()
    for copy in copies:
        copy.wait()
    weight = w_s[...]
    own = jnp.dot(keep_ref[...], weight, preferred_element_type=F32)
    own = (row_s[0] * own).astype(BF16)
    other = jnp.dot(got_ref[...], weight, preferred_element_type=F32)
    other = (row_s[1] * other).astype(BF16)
    own_ref[...] = own
    other_ref[...] = other
    total_ref[...] = (
        size_ref[own_index] * own.astype(F32) + size_ref[other_index] * other.astype(F32)
    ).astype(BF16)


def output(where, step_index, step_sizes, keep, got, table, pieces):
    half, feats = keep.shape
    width = table.shape[2]
    any_spec = pl.BlockSpec(memory_space=pl.ANY)
    vmem = pl.BlockSpec(memory_space=pltpu.VMEM)
    smem = pl.BlockSpec(memory_space=pltpu.SMEM)
    return pl.pallas_call(
        output_kernel,
        in_specs=[smem, smem, smem, vmem, vmem] + [any_spec] * 5,
        out_specs=[vmem] * 3,
        scratch_shapes=[
            pltpu.VMEM((feats, width), BF16),
            pltpu.VMEM((2, 1, width), F32),
            pltpu.SemaphoreType.DMA((8,)),
            pltpu.SemaphoreType.DMA((2,)),
        ],
        out_shape=[jax.ShapeDtypeStruct((half, width), BF16)] * 3,
        compiler_params=pltpu.CompilerParams(vmem_limit_bytes=VMEM_LIMIT),
        name="output",
    )(where, step_index, step_sizes, keep, got, table, *pieces)


def earlier_kernel(where_ref, index_ref, size_ref, one_ref, two_ref, three_ref, own_ref, out_ref):
    core = where_ref[2]
    size = jnp.where(core == 0, size_ref[index_ref[where_ref[0]]], 0.0)
    total = one_ref[...].astype(F32) + two_ref[...].astype(F32) + three_ref[...].astype(F32)
    out_ref[...] = (total + size * own_ref[...].astype(F32)).astype(BF16)


def earlier_sum(where, step_index, step_sizes, one, two, three, own):
    vmem = pl.BlockSpec(memory_space=pltpu.VMEM)
    smem = pl.BlockSpec(memory_space=pltpu.SMEM)
    return pl.pallas_call(
        earlier_kernel,
        in_specs=[smem, smem, smem] + [vmem] * 4,
        out_specs=vmem,
        out_shape=jax.ShapeDtypeStruct(own.shape, BF16),
        name="earlier_sum",
    )(where, step_index, step_sizes, one, two, three, own)


def advance_kernel(
    where_ref,
    index_ref,
    size_ref,
    one_ref,
    two_ref,
    three_ref,
    own_ref,
    other_ref,
    before_ref,
    rest_ref,
    anchor_ref,
    velocity_ref,
    advanced_ref,
):
    step, core = where_ref[0], where_ref[2]
    half = own_ref.shape[0]
    size_own = size_ref[index_ref[step]]
    size_other = jnp.where(core == 1, size_ref[index_ref[step + 1 - 2 * core]], 0.0)
    near = pl.ds(pl.multiple_of(core * half, half), half)
    far = pl.ds(pl.multiple_of((1 - core) * half, half), half)
    own = own_ref[...]
    velocity_ref[near] = own
    total = one_ref[...].astype(F32) + two_ref[...].astype(F32) + three_ref[...].astype(F32)
    total = total + size_other * other_ref[...].astype(F32) + size_own * own.astype(F32)
    advanced_ref[near] = anchor_ref[near] + total
    rest = rest_ref[...]
    velocity_ref[far] = rest
    advanced_ref[far] = (
        anchor_ref[far] + before_ref[...].astype(F32) + size_own * rest.astype(F32)
    )


def advance(where, step_index, step_sizes, one, two, three, own, other, before, rest, anchor):
    vmem = pl.BlockSpec(memory_space=pltpu.VMEM)
    smem = pl.BlockSpec(memory_space=pltpu.SMEM)
    return pl.pallas_call(
        advance_kernel,
        in_specs=[smem, smem, smem] + [vmem] * 8,
        out_specs=[vmem] * 2,
        out_shape=[
            jax.ShapeDtypeStruct(anchor.shape, BF16),
            jax.ShapeDtypeStruct(anchor.shape, F32),
        ],
        name="advance",
    )(where, step_index, step_sizes, one, two, three, own, other, before, rest, anchor)


def placed_y(parts, own):
    result = jnp.zeros((NZ, NY, 8, parts[0].shape[1]), BF16)
    for i, part in enumerate(parts):
        part = part.reshape(NZ, 1, 8, -1)
        result = lax.dynamic_update_slice_in_dim(result, part, lax.rem(own + i, NY), 1)
    return result


def on_device(
    latents,
    anchor,
    step_index,
    modulation,
    step_sizes,
    input_weight,
    output_weight,
    norm_gain,
    block_mask,
):
    latent = latents[0]
    rows, width = latent.shape
    step = lax.axis_index("step")
    frame = lax.axis_index("frame")
    x, core = step // 2, lax.rem(step, 2)
    z, y = frame // NY, lax.rem(frame, NY)
    where_am_i = jnp.stack([step, x, core, frame]).astype(jnp.int32)

    table = jnp.transpose(modulation, (1, 0, 2))

    out_width = output_weight.shape[1]
    packed = jnp.concatenate([input_weight, output_weight.reshape(2, -1)], axis=0)
    modulated = modulate(where_am_i, step_index, latent, table)
    packed, modulated = lax.optimization_barrier((packed, modulated))
    zp, zm = z_shift(modulated, 1), z_shift(modulated, -1)
    two_a = y_shift(modulated, 2)
    columns_z = [[NY * i + j for i in range(NZ)] for j in range(NY)]
    column = lax.all_to_all(
        jnp.broadcast_to(packed[None], (NZ,) + packed.shape),
        "frame",
        0,
        0,
        axis_index_groups=columns_z,
    ).reshape(8 * NZ, -1)
    column, zp, zm, two_a = lax.optimization_barrier((column, zp, zm, two_a))

    zp2, zm2 = z_shift(zp, 1), z_shift(zm, -1)
    plane = placed_y([column] + [y_shift(column, -d) for d in range(1, NY)], y)
    plane, zp2, zm2 = lax.optimization_barrier((plane, zp2, zm2))
    in_rows = plane[:, :, :6].reshape(192, -1)
    out_rows = plane[:, :, 6:].reshape(96, out_width)

    left, right = x_shift(in_rows, 1), x_shift(in_rows, -1)

    before = y_shift(jnp.where(y == NY - 1, zp, modulated), 1)
    after = y_shift(jnp.where(y == 0, zm, modulated), -1)
    z4_top = z_shift(zp2[: rows // 2], 2)
    in_rows, out_rows, left, right, before, after, z4_top, zm2, zp, zm = lax.optimization_barrier(
        (in_rows, out_rows, left, right, before, after, z4_top, zm2, zp, zm)
    )
    far_top = x_shift(left[:96], 1)
    far_bottom = x_shift(right[96:], -1)
    z4_bottom = z_shift(zm2[rows // 2 :], -2)
    two_b = y_shift(jnp.where(y >= 2, zp, zm), 2)
    near = [core_swap(piece) for piece in (in_rows, left, right)]
    out_rows = jnp.stack([out_rows, core_swap(out_rows)])
    far_top, far_bottom, z4_bottom, two_b, out_rows = lax.optimization_barrier(
        (far_top, far_bottom, z4_bottom, two_b, out_rows)
    )
    slabs = [modulated, zp, zm, two_a, zp2, zm2, before, after, two_b, z4_top, z4_bottom]
    pieces = [in_rows, left, right, far_top, far_bottom]
    pieces = pieces + near + [core_swap(far_top), core_swap(far_bottom)]

    out_pieces = [out_rows, x_shift(out_rows, 1), x_shift(out_rows, -1), x_shift(out_rows, 2)]
    keep, send = attend(where_am_i, block_mask, norm_gain, slabs, pieces)

    got = core_swap(send)
    own, other, total = output(
        where_am_i, step_index, step_sizes, keep, got, table, out_pieces
    )
    one = x_later(total, 1)
    three = x_later(total, 3)
    two = x_later(one, 1)
    rest = core_swap(other)
    sums = earlier_sum(where_am_i, step_index, step_sizes, one, two, three, own)
    before = core_swap(sums)
    velocity, advanced = advance(
        where_am_i, step_index, step_sizes, one, two, three, own, other, before, rest, anchor
    )
    return (velocity[None], advanced[None])


def solution(mesh):
    placed = (
        P("step", "frame", None),
        P("frame", None),
        P(),
        P(),
        P(),
        P(("step", "frame"), None),
        P(("step", "frame"), None),
        P(),
        P("frame", None),
    )
    return jax.shard_map(
        on_device,
        mesh=mesh,
        in_specs=placed,
        out_specs=(P("step", "frame", None), P("step", "frame", None)),
        check_vma=False,
    )
```

```python
import functools
import math

import jax
import jax.numpy as jnp
from jax import lax
from jax.experimental import pallas as pl
from jax.experimental.pallas import tpu as pltpu
from jax.sharding import PartitionSpec as P

HD = 128
BLK = 128
NX, NY, NZ = 4, 4, 8
NORM_EPS = 1e-06
F32 = jnp.float32
BF16 = jnp.bfloat16
VMEM_LIMIT = 56 * 1024 * 1024


def y_shift(block, distance):
    pairs = [(4 * z + y, 4 * z + (y + distance) % NY) for z in range(NZ) for y in range(NY)]
    return lax.ppermute(block, "frame", pairs)


def z_shift(block, distance):
    pairs = [(4 * z + y, 4 * ((z + distance) % NZ) + y) for z in range(NZ) for y in range(NY)]
    return lax.ppermute(block, "frame", pairs)


def x_shift(block, distance):
    pairs = [(2 * x + c, 2 * ((x + distance) % NX) + c) for x in range(NX) for c in range(2)]
    return lax.ppermute(block, "step", pairs)


def x_later(block, distance):
    pairs = [(2 * x + c, 2 * (x + distance) + c) for x in range(NX - distance) for c in range(2)]
    return lax.ppermute(block, "step", pairs)


def core_swap(block):
    return lax.ppermute(block, "step", [(i, i ^ 1) for i in range(2 * NX)])


def modulate_kernel(where_ref, index_ref, latent_ref, table_ref, out_ref, row_s, sem):
    own = index_ref[where_ref[0]]
    copies = [
        pltpu.make_async_copy(table_ref.at[i, pl.ds(own, 1)], row_s.at[i], sem.at[i])
        for i in range(2)
    ]
    for copy in copies:
        copy.start()
    value = latent_ref[...].astype(F32)
    centered = value - jnp.mean(value, axis=-1, keepdims=True)
    variance = jnp.mean(centered * centered, axis=-1, keepdims=True)
    normed = centered * lax.rsqrt(variance + NORM_EPS)
    for copy in copies:
        copy.wait()
    out_ref[...] = (normed * (1.0 + row_s[1]) + row_s[0]).astype(BF16)


def modulate(where, step_index, latent, table):
    rows, width = latent.shape
    return pl.pallas_call(
        modulate_kernel,
        in_specs=[
            pl.BlockSpec(memory_space=pltpu.SMEM),
            pl.BlockSpec(memory_space=pltpu.SMEM),
            pl.BlockSpec(memory_space=pltpu.VMEM),
            pl.BlockSpec(memory_space=pl.ANY),
        ],
        out_specs=pl.BlockSpec(memory_space=pltpu.VMEM),
        out_shape=jax.ShapeDtypeStruct((rows, width), BF16),
        scratch_shapes=[pltpu.VMEM((2, 1, width), F32), pltpu.SemaphoreType.DMA((2,))],
        name="modulate",
    )(where, step_index, latent, table)


N_SLABS = 10


def attend_kernel(
    where_ref,
    mask_ref,
    gain_ref,
    *refs,
):
    slabs = refs[:9]
    z4_top, z4_bottom = refs[9:11]
    pieces = refs[11:19]
    keep_ref, send_ref = refs[19:21]
    m_s, w_s, k_s, v_s, q_s, bias_s, m_sem, w_sem = refs[21:]
    x, core, frame = where_ref[1], where_ref[2], where_ref[3]
    rows = q_s.shape[0]
    feats = q_s.shape[1]
    half = rows // 2

    copies_m = []
    for i in range(9):
        copies_m.append(pltpu.make_async_copy(slabs[i], m_s.at[pl.ds(i * rows, rows)], m_sem.at[i]))
    copies_m.append(pltpu.make_async_copy(z4_top, m_s.at[pl.ds(9 * rows, half)], m_sem.at[9]))
    copies_m.append(
        pltpu.make_async_copy(z4_bottom, m_s.at[pl.ds(9 * rows + half, half)], m_sem.at[10])
    )
    depth = w_s.shape[0] // (2 * NX)
    copies_w = []
    for who in range(2):
        for i, distance in enumerate((0, -1, 1, 2)):
            piece = pieces[who * 4 + i]
            from_x = lax.rem(x + distance + NX, NX)
            from_core = core if who == 0 else 1 - core
            start = pl.multiple_of((2 * from_x + from_core) * depth, 16)
            copies_w.append(
                pltpu.make_async_copy(
                    piece, w_s.at[pl.ds(start, depth)], w_sem.at[who * 4 + i]
                )
            )
    copies_m[0].start()
    for copy in copies_w:
        copy.start()
    for copy in copies_m[1:]:
        copy.start()

    low = lax.rem(frame, NY) < 2
    two_a = jnp.where(low, 2, -2)
    offsets = (0, -4, 4, two_a, -8, 8, -1, 1, -two_a)
    for i in range(N_SLABS):
        if i < 9:
            source = frame + offsets[i]
        else:
            source = lax.rem(frame + 16, 32)
        inside = jnp.logical_and(source >= 0, source < 32)
        source = jnp.clip(source, 0, 31)
        for q_block in range(2):
            for k_block in range(2):
                ok = jnp.logical_and(inside, mask_ref[q_block, 2 * source + k_block] > 0)
                bias_s[q_block : q_block + 1, pl.ds(i * rows + k_block * BLK, BLK)] = jnp.full(
                    (1, BLK), jnp.where(ok, 0.0, -jnp.inf), F32
                )

    def rms(value, gain):
        square = jnp.mean(value * value, axis=-1, keepdims=True)
        return (value * lax.rsqrt(square + NORM_EPS) * gain).astype(BF16)

    copies_m[0].wait()
    for copy in copies_w:
        copy.wait()
    projected = jnp.dot(m_s[0:rows], w_s[:, 0:feats], preferred_element_type=F32)
    q_s[...] = rms(projected, gain_ref[0:1, :])
    for copy in copies_m[1:]:
        copy.wait()

    span = 2 * rows

    def project(i, carry):
        at = pl.ds(pl.multiple_of(i * span, span), span)
        block = m_s[at]
        keys = jnp.dot(block, w_s[:, feats : 2 * feats], preferred_element_type=F32)
        k_s[at] = rms(keys, gain_ref[1:2, :])
        values = jnp.dot(block, w_s[:, 2 * feats :], preferred_element_type=F32)
        v_s[at] = values.astype(BF16)
        return carry

    lax.fori_loop(0, N_SLABS // 2, project, 0)

    factor = 1.0 / math.sqrt(HD)
    for out_ref, q_block in ((send_ref, 1 - core), (keep_ref, core)):
        at = pl.ds(pl.multiple_of(q_block * BLK, BLK), BLK)
        bias = bias_s[pl.ds(q_block, 1), :]
        for head in range(feats // HD):
            cols = slice(head * HD, (head + 1) * HD)
            scores = lax.dot_general(
                q_s[at, cols], k_s[:, cols], (((1,), (1,)), ((), ())), preferred_element_type=F32
            )
            scores = scores * factor + bias
            peak = jnp.max(scores, axis=-1, keepdims=True)
            terms = jnp.exp(scores - peak)
            total = jnp.sum(terms, axis=-1, keepdims=True)
            mixed = jnp.dot(terms.astype(BF16), v_s[:, cols], preferred_element_type=F32)
            out_ref[:, cols] = (mixed / total).astype(BF16)


def attend(where, block_mask, norm_gain, slabs, pieces):
    rows, width = slabs[0].shape
    feats = norm_gain.shape[1]
    keys = N_SLABS * rows
    any_spec = pl.BlockSpec(memory_space=pl.ANY)
    smem = pl.BlockSpec(memory_space=pltpu.SMEM)
    return pl.pallas_call(
        attend_kernel,
        in_specs=[smem, smem, pl.BlockSpec(memory_space=pltpu.VMEM)]
        + [any_spec] * (len(slabs) + len(pieces)),
        out_specs=[pl.BlockSpec(memory_space=pltpu.VMEM)] * 2,
        out_shape=[jax.ShapeDtypeStruct((BLK, feats), BF16)] * 2,
        scratch_shapes=[
            pltpu.VMEM((keys, width), BF16),
            pltpu.VMEM((width, 3 * feats), BF16),
            pltpu.VMEM((keys, feats), BF16),
            pltpu.VMEM((keys, feats), BF16),
            pltpu.VMEM((rows, feats), BF16),
            pltpu.VMEM((2, keys), F32),
            pltpu.SemaphoreType.DMA((11,)),
            pltpu.SemaphoreType.DMA((8,)),
        ],
        compiler_params=pltpu.CompilerParams(vmem_limit_bytes=VMEM_LIMIT),
        cost_estimate=pl.CostEstimate(
            flops=16_000_000_000, bytes_accessed=16_000_000, transcendentals=4_000_000
        ),
        name="attend",
    )(where, block_mask, norm_gain, *slabs, *pieces)


def output_kernel(where_ref, index_ref, size_ref, keep_ref, got_ref, table_ref, *refs):
    pieces = refs[:4]
    own_ref, other_ref, total_ref, w_s, row_s, sem, row_sem = refs[4:]
    step, x, core = where_ref[0], where_ref[1], where_ref[2]
    own_index = index_ref[step]
    other_index = index_ref[step + 1 - 2 * core]
    depth = w_s.shape[0] // (2 * NX)
    copies = []
    for who in range(2):
        for i, distance in enumerate((0, -1, 1, 2)):
            from_x = lax.rem(x + distance + NX, NX)
            from_core = core if who == 0 else 1 - core
            start = pl.multiple_of((2 * from_x + from_core) * depth, 16)
            copies.append(
                pltpu.make_async_copy(
                    pieces[i].at[who], w_s.at[pl.ds(start, depth)], sem.at[who * 4 + i]
                )
            )
    for i, index in enumerate((own_index, other_index)):
        copies.append(
            pltpu.make_async_copy(table_ref.at[2, pl.ds(index, 1)], row_s.at[i], row_sem.at[i])
        )
    for copy in copies:
        copy.start()
    for copy in copies:
        copy.wait()
    both = jnp.concatenate([keep_ref[...], got_ref[...]], axis=0)
    both = jnp.dot(both, w_s[...], preferred_element_type=F32)
    half = keep_ref.shape[0]
    own = (row_s[0] * both[:half]).astype(BF16)
    other = (row_s[1] * both[half:]).astype(BF16)
    own_ref[...] = own
    other_ref[...] = other
    total_ref[...] = (
        size_ref[own_index] * own.astype(F32) + size_ref[other_index] * other.astype(F32)
    ).astype(BF16)


def output(where, step_index, step_sizes, keep, got, table, pieces):
    half, feats = keep.shape
    width = table.shape[2]
    any_spec = pl.BlockSpec(memory_space=pl.ANY)
    vmem = pl.BlockSpec(memory_space=pltpu.VMEM)
    smem = pl.BlockSpec(memory_space=pltpu.SMEM)
    return pl.pallas_call(
        output_kernel,
        in_specs=[smem, smem, smem, vmem, vmem] + [any_spec] * 5,
        out_specs=[vmem] * 3,
        scratch_shapes=[
            pltpu.VMEM((feats, width), BF16),
            pltpu.VMEM((2, 1, width), F32),
            pltpu.SemaphoreType.DMA((8,)),
            pltpu.SemaphoreType.DMA((2,)),
        ],
        out_shape=[jax.ShapeDtypeStruct((half, width), BF16)] * 3,
        compiler_params=pltpu.CompilerParams(vmem_limit_bytes=VMEM_LIMIT),
        name="output",
    )(where, step_index, step_sizes, keep, got, table, *pieces)


def base_kernel(
    where_ref,
    index_ref,
    size_ref,
    own_ref,
    other_ref,
    rest_ref,
    anchor_ref,
    velocity_ref,
    base_ref,
):
    step, core = where_ref[0], where_ref[2]
    near = pl.program_id(0) == core
    size_own = size_ref[index_ref[step]]
    size_other = jnp.where(
        jnp.logical_and(near, core == 1), size_ref[index_ref[step + 1 - 2 * core]], 0.0
    )
    value = jnp.where(near, own_ref[...].astype(F32), rest_ref[...].astype(F32))
    velocity_ref[...] = value.astype(BF16)
    base_ref[...] = (
        anchor_ref[...] + size_other * other_ref[...].astype(F32) + size_own * value
    )


def base(where, step_index, step_sizes, own, other, rest, anchor):
    half, width = own.shape
    smem = pl.BlockSpec(memory_space=pltpu.SMEM)
    part = pl.BlockSpec((half // 2, width), lambda i, j: (j, 0))
    whole = pl.BlockSpec((half // 2, width), lambda i, j: (2 * i + j, 0))
    return pl.pallas_call(
        base_kernel,
        grid=(2, 2),
        in_specs=[smem, smem, smem, part, part, part, whole],
        out_specs=[whole, whole],
        out_shape=[
            jax.ShapeDtypeStruct(anchor.shape, BF16),
            jax.ShapeDtypeStruct(anchor.shape, F32),
        ],
        cost_estimate=pl.CostEstimate(
            flops=3_000_000, bytes_accessed=6_000_000, transcendentals=0
        ),
        name="base",
    )(where, step_index, step_sizes, own, other, rest, anchor)


def add_kernel(where_ref, *refs):
    value = refs[0][...]
    for part_ref in refs[1:-1]:
        value = value + part_ref[...].astype(F32)
    refs[-1][...] = value


def add_half(where, near, value, parts, name):
    half, width = parts[0].shape

    def place(i, where):
        core = where[2] if near else 1 - where[2]
        return (2 * core + i, 0)

    return pl.pallas_call(
        add_kernel,
        grid_spec=pltpu.PrefetchScalarGridSpec(
            num_scalar_prefetch=1,
            grid=(2,),
            in_specs=[pl.BlockSpec((half // 2, width), place)]
            + [pl.BlockSpec((half // 2, width), lambda i, where: (i, 0))] * len(parts),
            out_specs=pl.BlockSpec((half // 2, width), place),
        ),
        out_shape=jax.ShapeDtypeStruct(value.shape, F32),
        input_output_aliases={1: 0},
        name=name,
    )(where, value, *parts)


def placed_y(parts, own):
    result = jnp.zeros((NZ, NY, 8, parts[0].shape[1]), BF16)
    for i, part in enumerate(parts):
        part = part.reshape(NZ, 1, 8, -1)
        result = lax.dynamic_update_slice_in_dim(result, part, lax.rem(own + i, NY), 1)
    return result


def on_device(
    latents,
    anchor,
    step_index,
    modulation,
    step_sizes,
    input_weight,
    output_weight,
    norm_gain,
    block_mask,
):
    latent = latents[0]
    rows, width = latent.shape
    step = lax.axis_index("step")
    frame = lax.axis_index("frame")
    x, core = step // 2, lax.rem(step, 2)
    z, y = frame // NY, lax.rem(frame, NY)
    where_am_i = jnp.stack([step, x, core, frame]).astype(jnp.int32)

    table = jnp.transpose(modulation, (1, 0, 2))

    size_own = step_sizes[step_index[step]]
    size_even = jnp.where(core == 0, size_own, 0.0)

    out_width = output_weight.shape[1]
    packed = jnp.concatenate([input_weight, output_weight.reshape(2, -1)], axis=0)
    columns_z = [[NY * i + j for i in range(NZ)] for j in range(NY)]
    column = lax.all_to_all(
        jnp.broadcast_to(packed[None], (NZ,) + packed.shape),
        "frame",
        0,
        0,
        axis_index_groups=columns_z,
    ).reshape(8 * NZ, -1)
    modulated = modulate(where_am_i, step_index, latent, table)
    two_a = y_shift(modulated, 2)
    column, modulated, size_even = lax.optimization_barrier((column, modulated, size_even))

    zp, zm = z_shift(modulated, 1), z_shift(modulated, -1)
    later, two_a = lax.optimization_barrier((column, two_a))
    plane = placed_y([column, y_shift(column, -1), y_shift(later, 2), y_shift(column, 1)], y)
    plane, zp, zm = lax.optimization_barrier((plane, zp, zm))
    in_rows = plane[:, :, :6].reshape(192, -1)
    out_rows = plane[:, :, 6:].reshape(96, out_width)

    left = x_shift(in_rows, 1)
    zp2, zm2 = z_shift(zp, 1), z_shift(zm, -1)
    before = y_shift(jnp.where(y == NY - 1, zp, modulated), 1)
    after = y_shift(jnp.where(y == 0, zm, modulated), -1)
    in_rows, out_rows, left, zp2, zm2, zp, zm, before, after = lax.optimization_barrier(
        (in_rows, out_rows, left, zp2, zm2, zp, zm, before, after)
    )

    right, far = x_shift(in_rows, -1), x_shift(left, 1)
    z4_top = z_shift(zp2[: rows // 2], 2)
    z4_bottom = z_shift(zm2[rows // 2 :], -2)
    two_b = y_shift(jnp.where(y >= 2, zp, zm), 2)
    near = [core_swap(piece) for piece in (in_rows, left)]
    out_rows = jnp.stack([out_rows, core_swap(out_rows)])
    right, far, z4_top, z4_bottom, two_b, out_rows = lax.optimization_barrier(
        (right, far, z4_top, z4_bottom, two_b, out_rows)
    )
    slabs = [modulated, zp, zm, two_a, zp2, zm2, before, after, two_b, z4_top, z4_bottom]
    pieces = [in_rows, left, right, far] + near + [core_swap(right), core_swap(far)]

    out_pieces = [out_rows, x_shift(out_rows, 1), x_shift(out_rows, -1), x_shift(out_rows, 2)]
    keep, send = attend(where_am_i, block_mask, norm_gain, slabs, pieces)

    got = core_swap(send)
    own, other, total = output(
        where_am_i, step_index, step_sizes, keep, got, table, out_pieces
    )
    one = x_later(total, 1)
    three = x_later(total, 3)
    two = x_later(one, 1)
    rest = core_swap(other)
    velocity, advanced = base(where_am_i, step_index, step_sizes, own, other, rest, anchor)
    two, velocity, advanced = lax.optimization_barrier((two, velocity, advanced))
    sums = one.astype(F32) + two.astype(F32) + three.astype(F32) + size_even * own.astype(F32)
    earlier = core_swap(sums.astype(BF16))
    advanced = add_half(where_am_i, True, advanced, [one, two, three], "add_near")
    advanced = add_half(where_am_i, False, advanced, [earlier], "add_far")
    return (velocity[None], advanced[None])


def solution(mesh):
    placed = (
        P("step", "frame", None),
        P("frame", None),
        P(),
        P(),
        P(),
        P(("step", "frame"), None),
        P(("step", "frame"), None),
        P(),
        P("frame", None),
    )
    return jax.shard_map(
        on_device,
        mesh=mesh,
        in_specs=placed,
        out_specs=(P("step", "frame", None), P("step", "frame", None)),
        check_vma=False,
    )
```

```python
import functools
import math

import jax
import jax.numpy as jnp
from jax import lax
from jax.experimental import pallas as pl
from jax.experimental.pallas import tpu as pltpu
from jax.sharding import PartitionSpec as P

HD = 128
BLK = 128
NX, NY, NZ = 4, 4, 8
NORM_EPS = 1e-06
F32 = jnp.float32
BF16 = jnp.bfloat16
VMEM_LIMIT = 56 * 1024 * 1024


def y_shift(block, distance):
    pairs = [(4 * z + y, 4 * z + (y + distance) % NY) for z in range(NZ) for y in range(NY)]
    return lax.ppermute(block, "frame", pairs)


def y_step(block, distance, edge):
    pairs = [(4 * z + y, 4 * z + (y + distance) % NY) for z in range(NZ) for y in range(NY)]
    pairs = [(i, j) for i, j in pairs if (i + distance != j) == edge]
    return lax.ppermute(block, "frame", pairs)


def z_shift(block, distance):
    pairs = [(4 * z + y, 4 * ((z + distance) % NZ) + y) for z in range(NZ) for y in range(NY)]
    return lax.ppermute(block, "frame", pairs)


def x_shift(block, distance):
    pairs = [(2 * x + c, 2 * ((x + distance) % NX) + c) for x in range(NX) for c in range(2)]
    return lax.ppermute(block, "step", pairs)


def x_later(block, distance):
    pairs = [(2 * x + c, 2 * (x + distance) + c) for x in range(NX - distance) for c in range(2)]
    return lax.ppermute(block, "step", pairs)


def core_swap(block):
    return lax.ppermute(block, "step", [(i, i ^ 1) for i in range(2 * NX)])


def modulate_kernel(where_ref, index_ref, latent_ref, table_ref, out_ref, row_s, sem):
    own = index_ref[where_ref[0]]
    copies = [
        pltpu.make_async_copy(table_ref.at[i, pl.ds(own, 1)], row_s.at[i], sem.at[i])
        for i in range(2)
    ]
    for copy in copies:
        copy.start()
    value = latent_ref[...].astype(F32)
    centered = value - jnp.mean(value, axis=-1, keepdims=True)
    variance = jnp.mean(centered * centered, axis=-1, keepdims=True)
    normed = centered * lax.rsqrt(variance + NORM_EPS)
    for copy in copies:
        copy.wait()
    out_ref[...] = (normed * (1.0 + row_s[1]) + row_s[0]).astype(BF16)


def modulate(where, step_index, latent, table):
    rows, width = latent.shape
    return pl.pallas_call(
        modulate_kernel,
        in_specs=[
            pl.BlockSpec(memory_space=pltpu.SMEM),
            pl.BlockSpec(memory_space=pltpu.SMEM),
            pl.BlockSpec(memory_space=pltpu.VMEM),
            pl.BlockSpec(memory_space=pl.ANY),
        ],
        out_specs=pl.BlockSpec(memory_space=pltpu.VMEM),
        out_shape=jax.ShapeDtypeStruct((rows, width), BF16),
        scratch_shapes=[pltpu.VMEM((2, 1, width), F32), pltpu.SemaphoreType.DMA((2,))],
        name="modulate",
    )(where, step_index, latent, table)


N_SLABS = 10


def attend_kernel(
    where_ref,
    mask_ref,
    gain_ref,
    *refs,
):
    slabs = refs[:9]
    z4_top, z4_bottom, before_edge, after_edge = refs[9:13]
    pieces = refs[13:23]
    keep_ref, send_ref = refs[23:25]
    m_s, w_s, k_s, v_s, q_s, bias_s, m_sem, w_sem = refs[25:]
    x, core, frame = where_ref[1], where_ref[2], where_ref[3]
    rows = q_s.shape[0]
    feats = q_s.shape[1]
    half = rows // 2

    copies_m = []
    for i in range(9):
        copies_m.append(pltpu.make_async_copy(slabs[i], m_s.at[pl.ds(i * rows, rows)], m_sem.at[i]))
    copies_m.append(pltpu.make_async_copy(z4_top, m_s.at[pl.ds(9 * rows, half)], m_sem.at[9]))
    copies_m.append(
        pltpu.make_async_copy(z4_bottom, m_s.at[pl.ds(9 * rows + half, half)], m_sem.at[10])
    )
    depth = w_s.shape[0] // (2 * NX)
    copies_w = []
    for who in range(2):
        for i, distance in enumerate((0, -1, 1, 2, 2)):
            piece = pieces[who * 5 + i]
            from_x = lax.rem(x + distance + NX, NX)
            from_core = core if who == 0 else 1 - core
            start = (2 * from_x + from_core) * depth
            if i == 4:
                start = start + depth // 2
            start = pl.multiple_of(start, 16)
            copies_w.append(
                pltpu.make_async_copy(
                    piece, w_s.at[pl.ds(start, piece.shape[0])], w_sem.at[who * 5 + i]
                )
            )
    copies_m[0].start()
    for copy in copies_w:
        copy.start()
    row_y = lax.rem(frame, NY)
    for i, edge_ref, at_edge in ((6, before_edge, 0), (7, after_edge, NY - 1)):
        edge_copy = pltpu.make_async_copy(
            edge_ref, m_s.at[pl.ds(i * rows, rows)], m_sem.at[i]
        )

        @pl.when(row_y == at_edge)
        def _():
            edge_copy.start()

        @pl.when(row_y != at_edge)
        def _():
            copies_m[i].start()

    for i, copy in enumerate(copies_m):
        if i not in (0, 6, 7):
            copy.start()

    low = lax.rem(frame, NY) < 2
    two_a = jnp.where(low, 2, -2)
    offsets = (0, -4, 4, two_a, -8, 8, -1, 1, -two_a)
    for i in range(N_SLABS):
        if i < 9:
            source = frame + offsets[i]
        else:
            source = lax.rem(frame + 16, 32)
        inside = jnp.logical_and(source >= 0, source < 32)
        source = jnp.clip(source, 0, 31)
        for q_block in range(2):
            for k_block in range(2):
                ok = jnp.logical_and(inside, mask_ref[q_block, 2 * source + k_block] > 0)
                bias_s[q_block : q_block + 1, pl.ds(i * rows + k_block * BLK, BLK)] = jnp.full(
                    (1, BLK), jnp.where(ok, 0.0, -jnp.inf), F32
                )

    def rms(value, gain):
        square = jnp.mean(value * value, axis=-1, keepdims=True)
        return (value * lax.rsqrt(square + NORM_EPS) * gain).astype(BF16)

    copies_m[0].wait()
    for copy in copies_w:
        copy.wait()
    projected = jnp.dot(m_s[0:rows], w_s[:, 0:feats], preferred_element_type=F32)
    q_s[...] = rms(projected, gain_ref[0:1, :])
    for copy in copies_m[1:]:
        copy.wait()

    span = 2 * rows

    def project(i, carry):
        at = pl.ds(pl.multiple_of(i * span, span), span)
        block = m_s[at]
        keys = jnp.dot(block, w_s[:, feats : 2 * feats], preferred_element_type=F32)
        k_s[at] = rms(keys, gain_ref[1:2, :])
        values = jnp.dot(block, w_s[:, 2 * feats :], preferred_element_type=F32)
        v_s[at] = values.astype(BF16)
        return carry

    lax.fori_loop(0, N_SLABS // 2, project, 0)

    factor = 1.0 / math.sqrt(HD)
    for out_ref, q_block in ((send_ref, 1 - core), (keep_ref, core)):
        at = pl.ds(pl.multiple_of(q_block * BLK, BLK), BLK)
        bias = bias_s[pl.ds(q_block, 1), :]
        for head in range(feats // HD):
            cols = slice(head * HD, (head + 1) * HD)
            scores = lax.dot_general(
                q_s[at, cols], k_s[:, cols], (((1,), (1,)), ((), ())), preferred_element_type=F32
            )
            scores = scores * factor + bias
            peak = jnp.max(scores, axis=-1, keepdims=True)
            terms = jnp.exp(scores - peak)
            total = jnp.sum(terms, axis=-1, keepdims=True)
            mixed = jnp.dot(terms.astype(BF16), v_s[:, cols], preferred_element_type=F32)
            out_ref[:, cols] = (mixed / total).astype(BF16)


def attend(where, block_mask, norm_gain, slabs, pieces):
    rows, width = slabs[0].shape
    feats = norm_gain.shape[1]
    keys = N_SLABS * rows
    any_spec = pl.BlockSpec(memory_space=pl.ANY)
    smem = pl.BlockSpec(memory_space=pltpu.SMEM)
    return pl.pallas_call(
        attend_kernel,
        in_specs=[smem, smem, pl.BlockSpec(memory_space=pltpu.VMEM)]
        + [any_spec] * (len(slabs) + len(pieces)),
        out_specs=[pl.BlockSpec(memory_space=pltpu.VMEM)] * 2,
        out_shape=[jax.ShapeDtypeStruct((BLK, feats), BF16)] * 2,
        scratch_shapes=[
            pltpu.VMEM((keys, width), BF16),
            pltpu.VMEM((width, 3 * feats), BF16),
            pltpu.VMEM((keys, feats), BF16),
            pltpu.VMEM((keys, feats), BF16),
            pltpu.VMEM((rows, feats), BF16),
            pltpu.VMEM((2, keys), F32),
            pltpu.SemaphoreType.DMA((11,)),
            pltpu.SemaphoreType.DMA((10,)),
        ],
        compiler_params=pltpu.CompilerParams(vmem_limit_bytes=VMEM_LIMIT),
        cost_estimate=pl.CostEstimate(
            flops=16_000_000_000, bytes_accessed=16_000_000, transcendentals=4_000_000
        ),
        name="attend",
    )(where, block_mask, norm_gain, *slabs, *pieces)


def output_kernel(where_ref, index_ref, size_ref, keep_ref, got_ref, table_ref, *refs):
    pieces = refs[:4]
    own_ref, other_ref, total_ref, w_s, row_s, sem, row_sem = refs[4:]
    step, x, core = where_ref[0], where_ref[1], where_ref[2]
    own_index = index_ref[step]
    other_index = index_ref[step + 1 - 2 * core]
    depth = w_s.shape[0] // (2 * NX)
    copies = []
    for who in range(2):
        for i, distance in enumerate((0, -1, 1, 2)):
            from_x = lax.rem(x + distance + NX, NX)
            from_core = core if who == 0 else 1 - core
            start = pl.multiple_of((2 * from_x + from_core) * depth, 16)
            copies.append(
                pltpu.make_async_copy(
                    pieces[i].at[who], w_s.at[pl.ds(start, depth)], sem.at[who * 4 + i]
                )
            )
    for i, index in enumerate((own_index, other_index)):
        copies.append(
            pltpu.make_async_copy(table_ref.at[2, pl.ds(index, 1)], row_s.at[i], row_sem.at[i])
        )
    for copy in copies:
        copy.start()
    for copy in copies:
        copy.wait()
    both = jnp.concatenate([keep_ref[...], got_ref[...]], axis=0)
    both = jnp.dot(both, w_s[...], preferred_element_type=F32)
    half = keep_ref.shape[0]
    own = (row_s[0] * both[:half]).astype(BF16)
    other = (row_s[1] * both[half:]).astype(BF16)
    own_ref[...] = own
    other_ref[...] = other
    total_ref[...] = (
        size_ref[own_index] * own.astype(F32) + size_ref[other_index] * other.astype(F32)
    ).astype(BF16)


def output(where, step_index, step_sizes, keep, got, table, pieces):
    half, feats = keep.shape
    width = table.shape[2]
    any_spec = pl.BlockSpec(memory_space=pl.ANY)
    vmem = pl.BlockSpec(memory_space=pltpu.VMEM)
    smem = pl.BlockSpec(memory_space=pltpu.SMEM)
    return pl.pallas_call(
        output_kernel,
        in_specs=[smem, smem, smem, vmem, vmem] + [any_spec] * 5,
        out_specs=[vmem] * 3,
        scratch_shapes=[
            pltpu.VMEM((feats, width), BF16),
            pltpu.VMEM((2, 1, width), F32),
            pltpu.SemaphoreType.DMA((8,)),
            pltpu.SemaphoreType.DMA((2,)),
        ],
        out_shape=[jax.ShapeDtypeStruct((half, width), BF16)] * 3,
        compiler_params=pltpu.CompilerParams(vmem_limit_bytes=VMEM_LIMIT),
        name="output",
    )(where, step_index, step_sizes, keep, got, table, *pieces)


def on_device(
    latents,
    anchor,
    step_index,
    modulation,
    step_sizes,
    input_weight,
    output_weight,
    norm_gain,
    block_mask,
):
    latent = latents[0]
    rows, width = latent.shape
    step = lax.axis_index("step")
    frame = lax.axis_index("frame")
    x, core = step // 2, lax.rem(step, 2)
    z, y = frame // NY, lax.rem(frame, NY)
    where_am_i = jnp.stack([step, x, core, frame]).astype(jnp.int32)

    table = jnp.transpose(modulation, (1, 0, 2))

    size_own = step_sizes[step_index[step]]
    size_other = step_sizes[step_index[step + 1 - 2 * core]]

    out_width = output_weight.shape[1]
    modulated = modulate(where_am_i, step_index, latent, table)
    input_weight, output_weight, modulated = lax.optimization_barrier(
        (input_weight, output_weight, modulated)
    )
    zp, zm = z_shift(modulated, 1), z_shift(modulated, -1)
    before = y_step(modulated, 1, False)
    after = y_step(modulated, -1, False)
    two_a = y_shift(modulated, 2)
    packed = jnp.concatenate([input_weight, output_weight.reshape(2, -1)], axis=0)
    columns_z = [[NY * i + j for i in range(NZ)] for j in range(NY)]
    column = lax.all_to_all(
        jnp.broadcast_to(packed[None], (NZ,) + packed.shape),
        "frame",
        0,
        0,
        axis_index_groups=columns_z,
    )
    column, zp, zm, before, after, two_a, size_own, size_other = lax.optimization_barrier(
        (column, zp, zm, before, after, two_a, size_own, size_other)
    )

    zp2, zm2 = z_shift(zp, 1), z_shift(zm, -1)
    before_edge = y_step(zp, 1, True)
    after_edge = y_step(zm, -1, True)
    rows_y = [[NY * i + j for j in range(NY)] for i in range(NZ)]
    plane = lax.all_to_all(
        jnp.broadcast_to(column[None], (NY,) + column.shape),
        "frame",
        0,
        0,
        axis_index_groups=rows_y,
    )
    plane, before_edge, after_edge, zp, zm = lax.optimization_barrier(
        (plane, before_edge, after_edge, zp, zm)
    )
    plane = jnp.transpose(plane, (1, 0, 2, 3))
    in_rows = plane[:, :, :6].reshape(192, -1)
    out_rows = plane[:, :, 6:].reshape(96, out_width)

    left, right = x_shift(in_rows, 1), x_shift(in_rows, -1)
    z4_top = z_shift(zp2[: rows // 2], 2)
    z4_bottom = z_shift(zm2[rows // 2 :], -2)
    two_b = y_shift(jnp.where(y >= 2, zp, zm), 2)
    in_rows, out_rows, left, right, z4_top, z4_bottom, two_b = lax.optimization_barrier(
        (in_rows, out_rows, left, right, z4_top, z4_bottom, two_b)
    )

    far_top = x_shift(left[:96], 1)
    far_bottom = x_shift(right[96:], -1)
    near = [core_swap(piece) for piece in (in_rows, left, right)]
    out_rows = jnp.stack([out_rows, core_swap(out_rows)])
    far_top, far_bottom, out_rows = lax.optimization_barrier((far_top, far_bottom, out_rows))
    slabs = [modulated, zp, zm, two_a, zp2, zm2, before, after, two_b, z4_top, z4_bottom]
    slabs = slabs + [before_edge, after_edge]
    pieces = [in_rows, left, right, far_top, far_bottom]
    pieces = pieces + near + [core_swap(far_top), core_swap(far_bottom)]

    out_pieces = [out_rows, x_shift(out_rows, 1), x_shift(out_rows, -1), x_shift(out_rows, 2)]
    keep, send = attend(where_am_i, block_mask, norm_gain, slabs, pieces)

    got = core_swap(send)
    own, other, total = output(
        where_am_i, step_index, step_sizes, keep, got, table, out_pieces
    )
    one = x_later(total, 1)
    three = x_later(total, 3)
    two = x_later(one, 1)
    rest = core_swap(other)
    parts = (2, rows // 2, width)
    near_half = (jnp.arange(2, dtype=jnp.int32) == core)[:, None, None]
    own32 = own.astype(F32)
    velocity = jnp.where(near_half, own[None], rest[None]).reshape(rows, width)
    sums = one.astype(F32) + two.astype(F32) + three.astype(F32)
    even = jnp.where(core == 0, size_own, 0.0)
    earlier = core_swap((sums + even * own32).astype(BF16))
    odd = jnp.where(core == 1, size_other, 0.0)
    own_part = sums + odd * other.astype(F32) + size_own * own32
    rest_part = earlier.astype(F32) + size_own * rest.astype(F32)
    advanced = anchor.reshape(parts) + jnp.where(near_half, own_part[None], rest_part[None])
    advanced = advanced.reshape(rows, width)
    return (velocity[None], advanced[None])


def solution(mesh):
    placed = (
        P("step", "frame", None),
        P("frame", None),
        P(),
        P(),
        P(),
        P(("step", "frame"), None),
        P(("step", "frame"), None),
        P(),
        P("frame", None),
    )
    return jax.shard_map(
        on_device,
        mesh=mesh,
        in_specs=placed,
        out_specs=(P("step", "frame", None), P("step", "frame", None)),
        check_vma=False,
    )
```

```python
import functools
import math

import jax
import jax.numpy as jnp
from jax import lax
from jax.experimental import pallas as pl
from jax.experimental.pallas import tpu as pltpu
from jax.sharding import PartitionSpec as P

HD = 128
BLK = 128
NX, NY, NZ = 4, 4, 8
NORM_EPS = 1e-06
F32 = jnp.float32
BF16 = jnp.bfloat16
VMEM_LIMIT = 56 * 1024 * 1024


def y_shift(block, distance):
    pairs = [(4 * z + y, 4 * z + (y + distance) % NY) for z in range(NZ) for y in range(NY)]
    return lax.ppermute(block, "frame", pairs)


def z_shift(block, distance):
    pairs = [(4 * z + y, 4 * ((z + distance) % NZ) + y) for z in range(NZ) for y in range(NY)]
    return lax.ppermute(block, "frame", pairs)


def x_shift(block, distance):
    pairs = [(2 * x + c, 2 * ((x + distance) % NX) + c) for x in range(NX) for c in range(2)]
    return lax.ppermute(block, "step", pairs)


def x_later(block, distance):
    pairs = [(2 * x + c, 2 * (x + distance) + c) for x in range(NX - distance) for c in range(2)]
    return lax.ppermute(block, "step", pairs)


def core_swap(block):
    return lax.ppermute(block, "step", [(i, i ^ 1) for i in range(2 * NX)])


def modulate_kernel(where_ref, index_ref, latent_ref, table_ref, out_ref, row_s, sem):
    own = index_ref[where_ref[0]]
    copies = [
        pltpu.make_async_copy(table_ref.at[i, pl.ds(own, 1)], row_s.at[i], sem.at[i])
        for i in range(2)
    ]
    for copy in copies:
        copy.start()
    value = latent_ref[...].astype(F32)
    centered = value - jnp.mean(value, axis=-1, keepdims=True)
    variance = jnp.mean(centered * centered, axis=-1, keepdims=True)
    normed = centered * lax.rsqrt(variance + NORM_EPS)
    for copy in copies:
        copy.wait()
    out_ref[...] = (normed * (1.0 + row_s[1]) + row_s[0]).astype(BF16)


def modulate(where, step_index, latent, table):
    rows, width = latent.shape
    return pl.pallas_call(
        modulate_kernel,
        in_specs=[
            pl.BlockSpec(memory_space=pltpu.SMEM),
            pl.BlockSpec(memory_space=pltpu.SMEM),
            pl.BlockSpec(memory_space=pltpu.VMEM),
            pl.BlockSpec(memory_space=pl.ANY),
        ],
        out_specs=pl.BlockSpec(memory_space=pltpu.VMEM),
        out_shape=jax.ShapeDtypeStruct((rows, width), BF16),
        scratch_shapes=[pltpu.VMEM((2, 1, width), F32), pltpu.SemaphoreType.DMA((2,))],
        name="modulate",
    )(where, step_index, latent, table)


N_SLABS = 10


def attend_kernel(
    where_ref,
    mask_ref,
    gain_ref,
    *refs,
):
    slabs = refs[:9]
    z4_top, z4_bottom = refs[9:11]
    pieces = refs[11:19]
    keep_ref, send_ref = refs[19:21]
    m_s, w_s, k_s, v_s, q_s, bias_s, m_sem, w_sem = refs[21:]
    x, core, frame = where_ref[1], where_ref[2], where_ref[3]
    rows = q_s.shape[0]
    feats = q_s.shape[1]
    half = rows // 2

    copies_m = []
    for i in range(9):
        copies_m.append(pltpu.make_async_copy(slabs[i], m_s.at[pl.ds(i * rows, rows)], m_sem.at[i]))
    copies_m.append(pltpu.make_async_copy(z4_top, m_s.at[pl.ds(9 * rows, half)], m_sem.at[9]))
    copies_m.append(
        pltpu.make_async_copy(z4_bottom, m_s.at[pl.ds(9 * rows + half, half)], m_sem.at[10])
    )
    depth = w_s.shape[0] // (2 * NX)
    copies_w = []
    for who in range(2):
        for i, distance in enumerate((0, -1, 1, 2)):
            piece = pieces[who * 4 + i]
            from_x = lax.rem(x + distance + NX, NX)
            from_core = core if who == 0 else 1 - core
            start = pl.multiple_of((2 * from_x + from_core) * depth, 16)
            copies_w.append(
                pltpu.make_async_copy(
                    piece, w_s.at[pl.ds(start, depth)], w_sem.at[who * 4 + i]
                )
            )
    copies_m[0].start()
    for copy in copies_w:
        copy.start()
    for copy in copies_m[1:]:
        copy.start()

    low = lax.rem(frame, NY) < 2
    two_a = jnp.where(low, 2, -2)
    offsets = (0, -4, 4, two_a, -8, 8, -1, 1, -two_a)
    for i in range(N_SLABS):
        if i < 9:
            source = frame + offsets[i]
        else:
            source = lax.rem(frame + 16, 32)
        inside = jnp.logical_and(source >= 0, source < 32)
        source = jnp.clip(source, 0, 31)
        for q_block in range(2):
            for k_block in range(2):
                ok = jnp.logical_and(inside, mask_ref[q_block, 2 * source + k_block] > 0)
                bias_s[q_block : q_block + 1, pl.ds(i * rows + k_block * BLK, BLK)] = jnp.full(
                    (1, BLK), jnp.where(ok, 0.0, -jnp.inf), F32
                )

    def rms(value, gain):
        square = jnp.mean(value * value, axis=-1, keepdims=True)
        return (value * lax.rsqrt(square + NORM_EPS) * gain).astype(BF16)

    copies_m[0].wait()
    for copy in copies_w:
        copy.wait()
    projected = jnp.dot(m_s[0:rows], w_s[:, 0:feats], preferred_element_type=F32)
    q_s[...] = rms(projected, gain_ref[0:1, :])
    for copy in copies_m[1:]:
        copy.wait()

    span = 2 * rows

    def project(i, carry):
        at = pl.ds(pl.multiple_of(i * span, span), span)
        block = m_s[at]
        keys = jnp.dot(block, w_s[:, feats : 2 * feats], preferred_element_type=F32)
        k_s[at] = rms(keys, gain_ref[1:2, :])
        values = jnp.dot(block, w_s[:, 2 * feats :], preferred_element_type=F32)
        v_s[at] = values.astype(BF16)
        return carry

    lax.fori_loop(0, N_SLABS // 2, project, 0)

    factor = 1.0 / math.sqrt(HD)
    for out_ref, q_block in ((send_ref, 1 - core), (keep_ref, core)):
        at = pl.ds(pl.multiple_of(q_block * BLK, BLK), BLK)
        bias = bias_s[pl.ds(q_block, 1), :]
        for head in range(feats // HD):
            cols = slice(head * HD, (head + 1) * HD)
            scores = lax.dot_general(
                q_s[at, cols], k_s[:, cols], (((1,), (1,)), ((), ())), preferred_element_type=F32
            )
            scores = scores * factor + bias
            peak = jnp.max(scores, axis=-1, keepdims=True)
            terms = jnp.exp(scores - peak)
            total = jnp.sum(terms, axis=-1, keepdims=True)
            mixed = jnp.dot(terms.astype(BF16), v_s[:, cols], preferred_element_type=F32)
            out_ref[:, cols] = (mixed / total).astype(BF16)


def attend(where, block_mask, norm_gain, slabs, pieces):
    rows, width = slabs[0].shape
    feats = norm_gain.shape[1]
    keys = N_SLABS * rows
    any_spec = pl.BlockSpec(memory_space=pl.ANY)
    smem = pl.BlockSpec(memory_space=pltpu.SMEM)
    return pl.pallas_call(
        attend_kernel,
        in_specs=[smem, smem, pl.BlockSpec(memory_space=pltpu.VMEM)]
        + [any_spec] * (len(slabs) + len(pieces)),
        out_specs=[pl.BlockSpec(memory_space=pltpu.VMEM)] * 2,
        out_shape=[jax.ShapeDtypeStruct((BLK, feats), BF16)] * 2,
        scratch_shapes=[
            pltpu.VMEM((keys, width), BF16),
            pltpu.VMEM((width, 3 * feats), BF16),
            pltpu.VMEM((keys, feats), BF16),
            pltpu.VMEM((keys, feats), BF16),
            pltpu.VMEM((rows, feats), BF16),
            pltpu.VMEM((2, keys), F32),
            pltpu.SemaphoreType.DMA((11,)),
            pltpu.SemaphoreType.DMA((8,)),
        ],
        compiler_params=pltpu.CompilerParams(vmem_limit_bytes=VMEM_LIMIT),
        cost_estimate=pl.CostEstimate(
            flops=16_000_000_000, bytes_accessed=16_000_000, transcendentals=4_000_000
        ),
        name="attend",
    )(where, block_mask, norm_gain, *slabs, *pieces)


def output_kernel(where_ref, index_ref, size_ref, keep_ref, got_ref, table_ref, *refs):
    pieces = refs[:4]
    own_ref, other_ref, total_ref, w_s, row_s, sem, row_sem = refs[4:]
    step, x, core = where_ref[0], where_ref[1], where_ref[2]
    own_index = index_ref[step]
    other_index = index_ref[step + 1 - 2 * core]
    depth = w_s.shape[0] // (2 * NX)
    copies = []
    for who in range(2):
        for i, distance in enumerate((0, -1, 1, 2)):
            from_x = lax.rem(x + distance + NX, NX)
            from_core = core if who == 0 else 1 - core
            start = pl.multiple_of((2 * from_x + from_core) * depth, 16)
            copies.append(
                pltpu.make_async_copy(
                    pieces[i].at[who], w_s.at[pl.ds(start, depth)], sem.at[who * 4 + i]
                )
            )
    for i, index in enumerate((own_index, other_index)):
        copies.append(
            pltpu.make_async_copy(table_ref.at[2, pl.ds(index, 1)], row_s.at[i], row_sem.at[i])
        )
    for copy in copies:
        copy.start()
    for copy in copies:
        copy.wait()
    both = jnp.concatenate([keep_ref[...], got_ref[...]], axis=0)
    both = jnp.dot(both, w_s[...], preferred_element_type=F32)
    half = keep_ref.shape[0]
    own = (row_s[0] * both[:half]).astype(BF16)
    other = (row_s[1] * both[half:]).astype(BF16)
    own_ref[...] = own
    other_ref[...] = other
    total_ref[...] = (
        size_ref[own_index] * own.astype(F32) + size_ref[other_index] * other.astype(F32)
    ).astype(BF16)


def output(where, step_index, step_sizes, keep, got, table, pieces):
    half, feats = keep.shape
    width = table.shape[2]
    any_spec = pl.BlockSpec(memory_space=pl.ANY)
    vmem = pl.BlockSpec(memory_space=pltpu.VMEM)
    smem = pl.BlockSpec(memory_space=pltpu.SMEM)
    return pl.pallas_call(
        output_kernel,
        in_specs=[smem, smem, smem, vmem, vmem] + [any_spec] * 5,
        out_specs=[vmem] * 3,
        scratch_shapes=[
            pltpu.VMEM((feats, width), BF16),
            pltpu.VMEM((2, 1, width), F32),
            pltpu.SemaphoreType.DMA((8,)),
            pltpu.SemaphoreType.DMA((2,)),
        ],
        out_shape=[jax.ShapeDtypeStruct((half, width), BF16)] * 3,
        compiler_params=pltpu.CompilerParams(vmem_limit_bytes=VMEM_LIMIT),
        name="output",
    )(where, step_index, step_sizes, keep, got, table, *pieces)


def placed_y(parts, own):
    result = jnp.zeros((NZ, NY, 8, parts[0].shape[1]), BF16)
    for i, part in enumerate(parts):
        part = part.reshape(NZ, 1, 8, -1)
        result = lax.dynamic_update_slice_in_dim(result, part, lax.rem(own + i, NY), 1)
    return result


def on_device(
    latents,
    anchor,
    step_index,
    modulation,
    step_sizes,
    input_weight,
    output_weight,
    norm_gain,
    block_mask,
):
    latent = latents[0]
    rows, width = latent.shape
    step = lax.axis_index("step")
    frame = lax.axis_index("frame")
    x, core = step // 2, lax.rem(step, 2)
    z, y = frame // NY, lax.rem(frame, NY)
    where_am_i = jnp.stack([step, x, core, frame]).astype(jnp.int32)

    table = jnp.transpose(modulation, (1, 0, 2))

    size_own = step_sizes[step_index[step]]
    size_other = step_sizes[step_index[step + 1 - 2 * core]]

    out_width = output_weight.shape[1]
    modulated = modulate(where_am_i, step_index, latent, table)
    input_weight, output_weight, modulated = lax.optimization_barrier(
        (input_weight, output_weight, modulated)
    )
    two_a = y_shift(modulated, 2)
    packed = jnp.concatenate([input_weight, output_weight.reshape(2, -1)], axis=0)
    columns_z = [[NY * i + j for i in range(NZ)] for j in range(NY)]
    column = lax.all_to_all(
        jnp.broadcast_to(packed[None], (NZ,) + packed.shape),
        "frame",
        0,
        0,
        axis_index_groups=columns_z,
    ).reshape(8 * NZ, -1)
    column, modulated, two_a, size_own, size_other = lax.optimization_barrier(
        (column, modulated, two_a, size_own, size_other)
    )

    zp, zm = z_shift(modulated, 1), z_shift(modulated, -1)
    plane = placed_y([column] + [y_shift(column, -d) for d in range(1, NY)], y)
    plane, zp, zm = lax.optimization_barrier((plane, zp, zm))
    in_rows = plane[:, :, :6].reshape(192, -1)
    out_rows = plane[:, :, 6:].reshape(96, out_width)

    left = x_shift(in_rows, 1)
    zp2, zm2 = z_shift(zp, 1), z_shift(zm, -1)
    before = y_shift(jnp.where(y == NY - 1, zp, modulated), 1)
    after = y_shift(jnp.where(y == 0, zm, modulated), -1)
    in_rows, out_rows, left, zp2, zm2, zp, zm, before, after = lax.optimization_barrier(
        (in_rows, out_rows, left, zp2, zm2, zp, zm, before, after)
    )

    right, far = x_shift(in_rows, -1), x_shift(left, 1)
    z4_top = z_shift(zp2[: rows // 2], 2)
    z4_bottom = z_shift(zm2[rows // 2 :], -2)
    two_b = y_shift(jnp.where(y >= 2, zp, zm), 2)
    near = [core_swap(piece) for piece in (in_rows, left)]
    out_rows = jnp.stack([out_rows, core_swap(out_rows)])
    right, far, z4_top, z4_bottom, two_b, out_rows = lax.optimization_barrier(
        (right, far, z4_top, z4_bottom, two_b, out_rows)
    )
    slabs = [modulated, zp, zm, two_a, zp2, zm2, before, after, two_b, z4_top, z4_bottom]
    pieces = [in_rows, left, right, far] + near + [core_swap(right), core_swap(far)]

    out_pieces = [out_rows, x_shift(out_rows, 1), x_shift(out_rows, -1), x_shift(out_rows, 2)]
    keep, send = attend(where_am_i, block_mask, norm_gain, slabs, pieces)

    got = core_swap(send)
    own, other, total = output(
        where_am_i, step_index, step_sizes, keep, got, table, out_pieces
    )
    one = x_later(total, 1)
    three = x_later(total, 3)
    two = x_later(one, 1)
    rest = core_swap(other)
    parts = (2, rows // 2, width)
    near_half = (jnp.arange(2, dtype=jnp.int32) == core)[:, None, None]
    own32 = own.astype(F32)
    velocity = jnp.where(near_half, own[None], rest[None]).reshape(rows, width)
    two, velocity = lax.optimization_barrier((two, velocity))
    even = jnp.where(core == 0, size_own, 0.0)
    odd = jnp.where(core == 1, size_other, 0.0)
    sums = one.astype(F32) + two.astype(F32) + three.astype(F32)
    earlier = core_swap((sums + even * own32).astype(BF16))
    one, two, three, own = lax.optimization_barrier((one, two, three, own))
    sums = one.astype(F32) + two.astype(F32) + three.astype(F32)
    own_part = sums + odd * other.astype(F32) + size_own * own.astype(F32)
    rest_part = earlier.astype(F32) + size_own * rest.astype(F32)
    advanced = anchor.reshape(parts) + jnp.where(near_half, own_part[None], rest_part[None])
    advanced = advanced.reshape(rows, width)
    return (velocity[None], advanced[None])


def solution(mesh):
    placed = (
        P("step", "frame", None),
        P("frame", None),
        P(),
        P(),
        P(),
        P(("step", "frame"), None),
        P(("step", "frame"), None),
        P(),
        P("frame", None),
    )
    return jax.shard_map(
        on_device,
        mesh=mesh,
        in_specs=placed,
        out_specs=(P("step", "frame", None), P("step", "frame", None)),
        check_vma=False,
    )
```

```python
import functools
import math

import jax
import jax.numpy as jnp
from jax import lax
from jax.experimental import pallas as pl
from jax.experimental.pallas import tpu as pltpu
from jax.sharding import PartitionSpec as P

HD = 128
BLK = 128
NX, NY, NZ = 4, 4, 8
NORM_EPS = 1e-06
F32 = jnp.float32
BF16 = jnp.bfloat16
ATTEND_VMEM = 40 * 1024 * 1024
OUTPUT_VMEM = 16 * 1024 * 1024


def y_shift(block, distance):
    pairs = [(4 * z + y, 4 * z + (y + distance) % NY) for z in range(NZ) for y in range(NY)]
    return lax.ppermute(block, "frame", pairs)


def z_shift(block, distance):
    pairs = [(4 * z + y, 4 * ((z + distance) % NZ) + y) for z in range(NZ) for y in range(NY)]
    return lax.ppermute(block, "frame", pairs)


def x_shift(block, distance):
    pairs = [(2 * x + c, 2 * ((x + distance) % NX) + c) for x in range(NX) for c in range(2)]
    return lax.ppermute(block, "step", pairs)


def x_later(block, distance):
    pairs = [(2 * x + c, 2 * (x + distance) + c) for x in range(NX - distance) for c in range(2)]
    return lax.ppermute(block, "step", pairs)


def core_swap(block):
    return lax.ppermute(block, "step", [(i, i ^ 1) for i in range(2 * NX)])


def modulate_kernel(where_ref, index_ref, latent_ref, table_ref, out_ref, row_s, sem):
    own = index_ref[where_ref[0]]
    copies = [
        pltpu.make_async_copy(table_ref.at[i, pl.ds(own, 1)], row_s.at[i], sem.at[i])
        for i in range(2)
    ]
    for copy in copies:
        copy.start()
    value = latent_ref[...].astype(F32)
    centered = value - jnp.mean(value, axis=-1, keepdims=True)
    variance = jnp.mean(centered * centered, axis=-1, keepdims=True)
    normed = centered * lax.rsqrt(variance + NORM_EPS)
    for copy in copies:
        copy.wait()
    out_ref[...] = (normed * (1.0 + row_s[1]) + row_s[0]).astype(BF16)


def modulate(where, step_index, latent, table):
    rows, width = latent.shape
    return pl.pallas_call(
        modulate_kernel,
        in_specs=[
            pl.BlockSpec(memory_space=pltpu.SMEM),
            pl.BlockSpec(memory_space=pltpu.SMEM),
            pl.BlockSpec(memory_space=pltpu.VMEM),
            pl.BlockSpec(memory_space=pl.ANY),
        ],
        out_specs=pl.BlockSpec(memory_space=pltpu.VMEM),
        out_shape=jax.ShapeDtypeStruct((rows, width), BF16),
        scratch_shapes=[pltpu.VMEM((2, 1, width), F32), pltpu.SemaphoreType.DMA((2,))],
        compiler_params=pltpu.CompilerParams(vmem_limit_bytes=OUTPUT_VMEM),
        name="modulate",
    )(where, step_index, latent, table)


N_SLABS = 10


def attend_kernel(
    where_ref,
    mask_ref,
    gain_ref,
    *refs,
):
    slabs = refs[:9]
    z4_top, z4_bottom = refs[9:11]
    pieces = refs[11:19]
    keep_ref, send_ref = refs[19:21]
    m_s, w_s, k_s, v_s, q_s, bias_s, m_sem, w_sem = refs[21:]
    x, core, frame = where_ref[1], where_ref[2], where_ref[3]
    rows = q_s.shape[0]
    feats = q_s.shape[1]
    half = rows // 2

    copies_m = []
    for i in range(9):
        copies_m.append(pltpu.make_async_copy(slabs[i], m_s.at[pl.ds(i * rows, rows)], m_sem.at[i]))
    copies_m.append(pltpu.make_async_copy(z4_top, m_s.at[pl.ds(9 * rows, half)], m_sem.at[9]))
    copies_m.append(
        pltpu.make_async_copy(z4_bottom, m_s.at[pl.ds(9 * rows + half, half)], m_sem.at[10])
    )
    depth = w_s.shape[0] // (2 * NX)
    copies_w = []
    for who in range(2):
        for i, distance in enumerate((0, -1, 1, 2)):
            piece = pieces[who * 4 + i]
            from_x = lax.rem(x + distance + NX, NX)
            from_core = core if who == 0 else 1 - core
            start = pl.multiple_of((2 * from_x + from_core) * depth, 16)
            copies_w.append(
                pltpu.make_async_copy(
                    piece, w_s.at[pl.ds(start, depth)], w_sem.at[who * 4 + i]
                )
            )
    copies_m[0].start()
    for copy in copies_w:
        copy.start()
    for copy in copies_m[1:]:
        copy.start()

    low = lax.rem(frame, NY) < 2
    two_a = jnp.where(low, 2, -2)
    offsets = (0, -4, 4, two_a, -8, 8, -1, 1, -two_a)
    for i in range(N_SLABS):
        if i < 9:
            source = frame + offsets[i]
        else:
            source = lax.rem(frame + 16, 32)
        inside = jnp.logical_and(source >= 0, source < 32)
        source = jnp.clip(source, 0, 31)
        for q_block in range(2):
            for k_block in range(2):
                ok = jnp.logical_and(inside, mask_ref[q_block, 2 * source + k_block] > 0)
                bias_s[q_block : q_block + 1, pl.ds(i * rows + k_block * BLK, BLK)] = jnp.full(
                    (1, BLK), jnp.where(ok, 0.0, -jnp.inf), F32
                )

    def rms(value, gain):
        square = jnp.mean(value * value, axis=-1, keepdims=True)
        return (value * lax.rsqrt(square + NORM_EPS) * gain).astype(BF16)

    copies_m[0].wait()
    for copy in copies_w:
        copy.wait()
    projected = jnp.dot(m_s[0:rows], w_s[:, 0:feats], preferred_element_type=F32)
    q_s[...] = rms(projected, gain_ref[0:1, :])
    for copy in copies_m[1:]:
        copy.wait()

    span = 2 * rows

    def project(i, carry):
        at = pl.ds(pl.multiple_of(i * span, span), span)
        block = m_s[at]
        keys = jnp.dot(block, w_s[:, feats : 2 * feats], preferred_element_type=F32)
        k_s[at] = rms(keys, gain_ref[1:2, :])
        values = jnp.dot(block, w_s[:, 2 * feats :], preferred_element_type=F32)
        v_s[at] = values.astype(BF16)
        return carry

    lax.fori_loop(0, N_SLABS // 2, project, 0)

    factor = 1.0 / math.sqrt(HD)
    for out_ref, q_block in ((send_ref, 1 - core), (keep_ref, core)):
        at = pl.ds(pl.multiple_of(q_block * BLK, BLK), BLK)
        bias = bias_s[pl.ds(q_block, 1), :]
        for head in range(feats // HD):
            cols = slice(head * HD, (head + 1) * HD)
            scores = lax.dot_general(
                q_s[at, cols], k_s[:, cols], (((1,), (1,)), ((), ())), preferred_element_type=F32
            )
            scores = scores * factor + bias
            peak = jnp.max(scores, axis=-1, keepdims=True)
            terms = jnp.exp(scores - peak)
            total = jnp.sum(terms, axis=-1, keepdims=True)
            mixed = jnp.dot(terms.astype(BF16), v_s[:, cols], preferred_element_type=F32)
            out_ref[:, cols] = (mixed / total).astype(BF16)


def attend(where, block_mask, norm_gain, slabs, pieces):
    rows, width = slabs[0].shape
    feats = norm_gain.shape[1]
    keys = N_SLABS * rows
    any_spec = pl.BlockSpec(memory_space=pl.ANY)
    smem = pl.BlockSpec(memory_space=pltpu.SMEM)
    return pl.pallas_call(
        attend_kernel,
        in_specs=[smem, smem, pl.BlockSpec(memory_space=pltpu.VMEM)]
        + [any_spec] * (len(slabs) + len(pieces)),
        out_specs=[pl.BlockSpec(memory_space=pltpu.VMEM)] * 2,
        out_shape=[jax.ShapeDtypeStruct((BLK, feats), BF16)] * 2,
        scratch_shapes=[
            pltpu.VMEM((keys, width), BF16),
            pltpu.VMEM((width, 3 * feats), BF16),
            pltpu.VMEM((keys, feats), BF16),
            pltpu.VMEM((keys, feats), BF16),
            pltpu.VMEM((rows, feats), BF16),
            pltpu.VMEM((2, keys), F32),
            pltpu.SemaphoreType.DMA((11,)),
            pltpu.SemaphoreType.DMA((8,)),
        ],
        compiler_params=pltpu.CompilerParams(vmem_limit_bytes=ATTEND_VMEM),
        cost_estimate=pl.CostEstimate(
            flops=16_000_000_000, bytes_accessed=16_000_000, transcendentals=4_000_000
        ),
        name="attend",
    )(where, block_mask, norm_gain, *slabs, *pieces)


def output_kernel(where_ref, index_ref, size_ref, keep_ref, got_ref, table_ref, *refs):
    pieces = refs[:4]
    own_ref, other_ref, total_ref, w_s, row_s, sem, row_sem = refs[4:]
    step, x, core = where_ref[0], where_ref[1], where_ref[2]
    own_index = index_ref[step]
    other_index = index_ref[step + 1 - 2 * core]
    depth = w_s.shape[0] // (2 * NX)
    copies = []
    for who in range(2):
        for i, distance in enumerate((0, -1, 1, 2)):
            from_x = lax.rem(x + distance + NX, NX)
            from_core = core if who == 0 else 1 - core
            start = pl.multiple_of((2 * from_x + from_core) * depth, 16)
            copies.append(
                pltpu.make_async_copy(
                    pieces[i].at[who], w_s.at[pl.ds(start, depth)], sem.at[who * 4 + i]
                )
            )
    for i, index in enumerate((own_index, other_index)):
        copies.append(
            pltpu.make_async_copy(table_ref.at[2, pl.ds(index, 1)], row_s.at[i], row_sem.at[i])
        )
    for copy in copies:
        copy.start()
    for copy in copies:
        copy.wait()
    both = jnp.concatenate([keep_ref[...], got_ref[...]], axis=0)
    both = jnp.dot(both, w_s[...], preferred_element_type=F32)
    half = keep_ref.shape[0]
    own = (row_s[0] * both[:half]).astype(BF16)
    other = (row_s[1] * both[half:]).astype(BF16)
    own_ref[...] = own
    other_ref[...] = other
    total_ref[...] = (
        size_ref[own_index] * own.astype(F32) + size_ref[other_index] * other.astype(F32)
    ).astype(BF16)


def output(where, step_index, step_sizes, keep, got, table, pieces):
    half, feats = keep.shape
    width = table.shape[2]
    any_spec = pl.BlockSpec(memory_space=pl.ANY)
    vmem = pl.BlockSpec(memory_space=pltpu.VMEM)
    smem = pl.BlockSpec(memory_space=pltpu.SMEM)
    return pl.pallas_call(
        output_kernel,
        in_specs=[smem, smem, smem, vmem, vmem] + [any_spec] * 5,
        out_specs=[vmem] * 3,
        scratch_shapes=[
            pltpu.VMEM((feats, width), BF16),
            pltpu.VMEM((2, 1, width), F32),
            pltpu.SemaphoreType.DMA((8,)),
            pltpu.SemaphoreType.DMA((2,)),
        ],
        out_shape=[jax.ShapeDtypeStruct((half, width), BF16)] * 3,
        compiler_params=pltpu.CompilerParams(vmem_limit_bytes=OUTPUT_VMEM),
        name="output",
    )(where, step_index, step_sizes, keep, got, table, *pieces)


def placed_y(parts, own):
    result = jnp.zeros((NZ, NY, 8, parts[0].shape[1]), BF16)
    for i, part in enumerate(parts):
        part = part.reshape(NZ, 1, 8, -1)
        result = lax.dynamic_update_slice_in_dim(result, part, lax.rem(own + i, NY), 1)
    return result


def on_device(
    latents,
    anchor,
    step_index,
    modulation,
    step_sizes,
    input_weight,
    output_weight,
    norm_gain,
    block_mask,
):
    latent = latents[0]
    rows, width = latent.shape
    step = lax.axis_index("step")
    frame = lax.axis_index("frame")
    x, core = step // 2, lax.rem(step, 2)
    z, y = frame // NY, lax.rem(frame, NY)
    where_am_i = jnp.stack([step, x, core, frame]).astype(jnp.int32)

    table = jnp.transpose(modulation, (1, 0, 2))

    size_own = step_sizes[step_index[step]]
    size_other = step_sizes[step_index[step + 1 - 2 * core]]

    out_width = output_weight.shape[1]
    modulated = modulate(where_am_i, step_index, latent, table)
    input_weight, output_weight, modulated = lax.optimization_barrier(
        (input_weight, output_weight, modulated)
    )
    two_a = y_shift(modulated, 2)
    packed = jnp.concatenate([input_weight, output_weight.reshape(2, -1)], axis=0)
    columns_z = [[NY * i + j for i in range(NZ)] for j in range(NY)]
    column = lax.all_to_all(
        jnp.broadcast_to(packed[None], (NZ,) + packed.shape),
        "frame",
        0,
        0,
        axis_index_groups=columns_z,
    ).reshape(8 * NZ, -1)
    column, modulated, two_a, size_own, size_other = lax.optimization_barrier(
        (column, modulated, two_a, size_own, size_other)
    )

    zp, zm = z_shift(modulated, 1), z_shift(modulated, -1)
    plane = placed_y([column] + [y_shift(column, -d) for d in range(1, NY)], y)
    plane, zp, zm = lax.optimization_barrier((plane, zp, zm))
    in_rows = plane[:, :, :6].reshape(192, -1)
    out_rows = plane[:, :, 6:].reshape(96, out_width)

    left = x_shift(in_rows, 1)
    zp2, zm2 = z_shift(zp, 1), z_shift(zm, -1)
    before = y_shift(jnp.where(y == NY - 1, zp, modulated), 1)
    after = y_shift(jnp.where(y == 0, zm, modulated), -1)
    in_rows, out_rows, left, zp2, zm2, zp, zm, before, after = lax.optimization_barrier(
        (in_rows, out_rows, left, zp2, zm2, zp, zm, before, after)
    )

    right, far = x_shift(in_rows, -1), x_shift(left, 1)
    z4_top = z_shift(zp2[: rows // 2], 2)
    z4_bottom = z_shift(zm2[rows // 2 :], -2)
    two_b = y_shift(jnp.where(y >= 2, zp, zm), 2)
    near = [core_swap(piece) for piece in (in_rows, left)]
    out_rows = jnp.stack([out_rows, core_swap(out_rows)])
    right, far, z4_top, z4_bottom, two_b, out_rows = lax.optimization_barrier(
        (right, far, z4_top, z4_bottom, two_b, out_rows)
    )
    slabs = [modulated, zp, zm, two_a, zp2, zm2, before, after, two_b, z4_top, z4_bottom]
    pieces = [in_rows, left, right, far] + near + [core_swap(right), core_swap(far)]

    out_pieces = [out_rows, x_shift(out_rows, 1), x_shift(out_rows, -1), x_shift(out_rows, 2)]
    keep, send = attend(where_am_i, block_mask, norm_gain, slabs, pieces)

    got = core_swap(send)
    own, other, total = output(
        where_am_i, step_index, step_sizes, keep, got, table, out_pieces
    )
    one = x_later(total, 1)
    three = x_later(total, 3)
    two = x_later(total, 2)
    rest = core_swap(other)
    parts = (2, rows // 2, width)
    near_half = (jnp.arange(2, dtype=jnp.int32) == core)[:, None, None]
    own32 = own.astype(F32)
    velocity = jnp.where(near_half, own[None], rest[None]).reshape(rows, width)
    two, velocity = lax.optimization_barrier((two, velocity))
    even = jnp.where(core == 0, size_own, 0.0)
    odd = jnp.where(core == 1, size_other, 0.0)
    sums = one.astype(F32) + two.astype(F32) + three.astype(F32)
    earlier = core_swap((sums + even * own32).astype(BF16))
    one, two, three, own = lax.optimization_barrier((one, two, three, own))
    sums = one.astype(F32) + two.astype(F32) + three.astype(F32)
    own_part = sums + odd * other.astype(F32) + size_own * own.astype(F32)
    rest_part = earlier.astype(F32) + size_own * rest.astype(F32)
    advanced = anchor.reshape(parts) + jnp.where(near_half, own_part[None], rest_part[None])
    advanced = advanced.reshape(rows, width)
    return (velocity[None], advanced[None])


def solution(mesh):
    placed = (
        P("step", "frame", None),
        P("frame", None),
        P(),
        P(),
        P(),
        P(("step", "frame"), None),
        P(("step", "frame"), None),
        P(),
        P("frame", None),
    )
    return jax.shard_map(
        on_device,
        mesh=mesh,
        in_specs=placed,
        out_specs=(P("step", "frame", None), P("step", "frame", None)),
        check_vma=False,
    )
```

```python
import functools
import math

import jax
import jax.numpy as jnp
from jax import lax
from jax.experimental import pallas as pl
from jax.experimental.pallas import tpu as pltpu
from jax.sharding import PartitionSpec as P

HD = 128
BLK = 128
NX, NY, NZ = 4, 4, 8
NORM_EPS = 1e-06
F32 = jnp.float32
BF16 = jnp.bfloat16
ATTEND_VMEM = 40 * 1024 * 1024
OUTPUT_VMEM = 16 * 1024 * 1024


def y_shift(block, distance):
    pairs = [(4 * z + y, 4 * z + (y + distance) % NY) for z in range(NZ) for y in range(NY)]
    return lax.ppermute(block, "frame", pairs)


def z_shift(block, distance):
    pairs = [(4 * z + y, 4 * ((z + distance) % NZ) + y) for z in range(NZ) for y in range(NY)]
    return lax.ppermute(block, "frame", pairs)


def x_shift(block, distance):
    pairs = [(2 * x + c, 2 * ((x + distance) % NX) + c) for x in range(NX) for c in range(2)]
    return lax.ppermute(block, "step", pairs)


def x_later(block, distance):
    pairs = [(2 * x + c, 2 * (x + distance) + c) for x in range(NX - distance) for c in range(2)]
    return lax.ppermute(block, "step", pairs)


def core_swap(block):
    return lax.ppermute(block, "step", [(i, i ^ 1) for i in range(2 * NX)])


def modulate_kernel(where_ref, index_ref, latent_ref, table_ref, out_ref, row_s, sem):
    own = index_ref[where_ref[0]]
    copies = [
        pltpu.make_async_copy(table_ref.at[i, pl.ds(own, 1)], row_s.at[i], sem.at[i])
        for i in range(2)
    ]
    for copy in copies:
        copy.start()
    value = latent_ref[...].astype(F32)
    centered = value - jnp.mean(value, axis=-1, keepdims=True)
    variance = jnp.mean(centered * centered, axis=-1, keepdims=True)
    normed = centered * lax.rsqrt(variance + NORM_EPS)
    for copy in copies:
        copy.wait()
    out_ref[...] = (normed * (1.0 + row_s[1]) + row_s[0]).astype(BF16)


def modulate(where, step_index, latent, table):
    rows, width = latent.shape
    return pl.pallas_call(
        modulate_kernel,
        in_specs=[
            pl.BlockSpec(memory_space=pltpu.SMEM),
            pl.BlockSpec(memory_space=pltpu.SMEM),
            pl.BlockSpec(memory_space=pltpu.VMEM),
            pl.BlockSpec(memory_space=pl.ANY),
        ],
        out_specs=pl.BlockSpec(memory_space=pltpu.VMEM),
        out_shape=jax.ShapeDtypeStruct((rows, width), BF16),
        scratch_shapes=[pltpu.VMEM((2, 1, width), F32), pltpu.SemaphoreType.DMA((2,))],
        compiler_params=pltpu.CompilerParams(vmem_limit_bytes=OUTPUT_VMEM),
        name="modulate",
    )(where, step_index, latent, table)


N_SLABS = 10


def attend_kernel(
    where_ref,
    mask_ref,
    gain_ref,
    *refs,
):
    slabs = refs[:9]
    z4_top, z4_bottom = refs[9:11]
    pieces = refs[11:19]
    keep_ref, send_ref = refs[19:21]
    m_s, w_s, k_s, v_s, q_s, bias_s, m_sem, w_sem = refs[21:]
    x, core, frame = where_ref[1], where_ref[2], where_ref[3]
    rows = q_s.shape[0]
    feats = q_s.shape[1]
    half = rows // 2

    copies_m = []
    for i in range(9):
        copies_m.append(pltpu.make_async_copy(slabs[i], m_s.at[pl.ds(i * rows, rows)], m_sem.at[i]))
    copies_m.append(pltpu.make_async_copy(z4_top, m_s.at[pl.ds(9 * rows, half)], m_sem.at[9]))
    copies_m.append(
        pltpu.make_async_copy(z4_bottom, m_s.at[pl.ds(9 * rows + half, half)], m_sem.at[10])
    )
    depth = w_s.shape[0] // (2 * NX)
    copies_w = []
    for who in range(2):
        for i, distance in enumerate((0, -1, 1, 2)):
            piece = pieces[who * 4 + i]
            from_x = lax.rem(x + distance + NX, NX)
            from_core = core if who == 0 else 1 - core
            start = pl.multiple_of((2 * from_x + from_core) * depth, 16)
            copies_w.append(
                pltpu.make_async_copy(
                    piece, w_s.at[pl.ds(start, depth)], w_sem.at[who * 4 + i]
                )
            )
    copies_m[0].start()
    for copy in copies_w:
        copy.start()
    for copy in copies_m[1:]:
        copy.start()

    low = lax.rem(frame, NY) < 2
    two_a = jnp.where(low, 2, -2)
    offsets = (0, -4, 4, two_a, -8, 8, -1, 1, -two_a)
    for i in range(N_SLABS):
        if i < 9:
            source = frame + offsets[i]
        else:
            source = lax.rem(frame + 16, 32)
        inside = jnp.logical_and(source >= 0, source < 32)
        source = jnp.clip(source, 0, 31)
        for q_block in range(2):
            for k_block in range(2):
                ok = jnp.logical_and(inside, mask_ref[q_block, 2 * source + k_block] > 0)
                bias_s[q_block : q_block + 1, pl.ds(i * rows + k_block * BLK, BLK)] = jnp.full(
                    (1, BLK), jnp.where(ok, 0.0, -jnp.inf), F32
                )

    def rms(value, gain):
        square = jnp.mean(value * value, axis=-1, keepdims=True)
        return (value * lax.rsqrt(square + NORM_EPS) * gain).astype(BF16)

    copies_m[0].wait()
    for copy in copies_w:
        copy.wait()
    projected = jnp.dot(m_s[0:rows], w_s[:, 0:feats], preferred_element_type=F32)
    q_s[...] = rms(projected, gain_ref[0:1, :])
    for copy in copies_m[1:]:
        copy.wait()

    span = 2 * rows

    def project(i, carry):
        at = pl.ds(pl.multiple_of(i * span, span), span)
        block = m_s[at]
        keys = jnp.dot(block, w_s[:, feats : 2 * feats], preferred_element_type=F32)
        k_s[at] = rms(keys, gain_ref[1:2, :])
        values = jnp.dot(block, w_s[:, 2 * feats :], preferred_element_type=F32)
        v_s[at] = values.astype(BF16)
        return carry

    lax.fori_loop(0, N_SLABS // 2, project, 0)

    factor = 1.0 / math.sqrt(HD)
    for out_ref, q_block in ((send_ref, 1 - core), (keep_ref, core)):
        at = pl.ds(pl.multiple_of(q_block * BLK, BLK), BLK)
        bias = bias_s[pl.ds(q_block, 1), :]
        for head in range(feats // HD):
            cols = slice(head * HD, (head + 1) * HD)
            scores = lax.dot_general(
                q_s[at, cols], k_s[:, cols], (((1,), (1,)), ((), ())), preferred_element_type=F32
            )
            scores = scores * factor + bias
            peak = jnp.max(scores, axis=-1, keepdims=True)
            terms = jnp.exp(scores - peak)
            total = jnp.sum(terms, axis=-1, keepdims=True)
            mixed = jnp.dot(terms.astype(BF16), v_s[:, cols], preferred_element_type=F32)
            out_ref[:, cols] = (mixed / total).astype(BF16)


def attend(where, block_mask, norm_gain, slabs, pieces):
    rows, width = slabs[0].shape
    feats = norm_gain.shape[1]
    keys = N_SLABS * rows
    any_spec = pl.BlockSpec(memory_space=pl.ANY)
    smem = pl.BlockSpec(memory_space=pltpu.SMEM)
    return pl.pallas_call(
        attend_kernel,
        in_specs=[smem, smem, pl.BlockSpec(memory_space=pltpu.VMEM)]
        + [any_spec] * (len(slabs) + len(pieces)),
        out_specs=[pl.BlockSpec(memory_space=pltpu.VMEM)] * 2,
        out_shape=[jax.ShapeDtypeStruct((BLK, feats), BF16)] * 2,
        scratch_shapes=[
            pltpu.VMEM((keys, width), BF16),
            pltpu.VMEM((width, 3 * feats), BF16),
            pltpu.VMEM((keys, feats), BF16),
            pltpu.VMEM((keys, feats), BF16),
            pltpu.VMEM((rows, feats), BF16),
            pltpu.VMEM((2, keys), F32),
            pltpu.SemaphoreType.DMA((11,)),
            pltpu.SemaphoreType.DMA((8,)),
        ],
        compiler_params=pltpu.CompilerParams(vmem_limit_bytes=ATTEND_VMEM),
        cost_estimate=pl.CostEstimate(
            flops=16_000_000_000, bytes_accessed=16_000_000, transcendentals=4_000_000
        ),
        name="attend",
    )(where, block_mask, norm_gain, *slabs, *pieces)


def output_kernel(where_ref, index_ref, size_ref, keep_ref, got_ref, table_ref, *refs):
    pieces = refs[:4]
    own_ref, other_ref, total_ref, w_s, row_s, sem, row_sem = refs[4:]
    step, x, core = where_ref[0], where_ref[1], where_ref[2]
    own_index = index_ref[step]
    other_index = index_ref[step + 1 - 2 * core]
    depth = w_s.shape[0] // (2 * NX)
    copies = []
    for who in range(2):
        for i, distance in enumerate((0, -1, 1, 2)):
            from_x = lax.rem(x + distance + NX, NX)
            from_core = core if who == 0 else 1 - core
            start = pl.multiple_of((2 * from_x + from_core) * depth, 16)
            copies.append(
                pltpu.make_async_copy(
                    pieces[i].at[who], w_s.at[pl.ds(start, depth)], sem.at[who * 4 + i]
                )
            )
    for i, index in enumerate((own_index, other_index)):
        copies.append(
            pltpu.make_async_copy(table_ref.at[2, pl.ds(index, 1)], row_s.at[i], row_sem.at[i])
        )
    for copy in copies:
        copy.start()
    for copy in copies:
        copy.wait()
    both = jnp.concatenate([keep_ref[...], got_ref[...]], axis=0)
    both = jnp.dot(both, w_s[...], preferred_element_type=F32)
    half = keep_ref.shape[0]
    own = (row_s[0] * both[:half]).astype(BF16)
    other = (row_s[1] * both[half:]).astype(BF16)
    own_ref[...] = own
    other_ref[...] = other
    total_ref[...] = (
        size_ref[own_index] * own.astype(F32) + size_ref[other_index] * other.astype(F32)
    ).astype(BF16)


def output(where, step_index, step_sizes, keep, got, table, pieces):
    half, feats = keep.shape
    width = table.shape[2]
    any_spec = pl.BlockSpec(memory_space=pl.ANY)
    vmem = pl.BlockSpec(memory_space=pltpu.VMEM)
    smem = pl.BlockSpec(memory_space=pltpu.SMEM)
    return pl.pallas_call(
        output_kernel,
        in_specs=[smem, smem, smem, vmem, vmem] + [any_spec] * 5,
        out_specs=[vmem] * 3,
        scratch_shapes=[
            pltpu.VMEM((feats, width), BF16),
            pltpu.VMEM((2, 1, width), F32),
            pltpu.SemaphoreType.DMA((8,)),
            pltpu.SemaphoreType.DMA((2,)),
        ],
        out_shape=[jax.ShapeDtypeStruct((half, width), BF16)] * 3,
        compiler_params=pltpu.CompilerParams(vmem_limit_bytes=OUTPUT_VMEM),
        name="output",
    )(where, step_index, step_sizes, keep, got, table, *pieces)


def placed_y(parts, own):
    result = jnp.zeros((NZ, NY, 8, parts[0].shape[1]), BF16)
    for i, part in enumerate(parts):
        part = part.reshape(NZ, 1, 8, -1)
        result = lax.dynamic_update_slice_in_dim(result, part, lax.rem(own + i, NY), 1)
    return result


def on_device(
    latents,
    anchor,
    step_index,
    modulation,
    step_sizes,
    input_weight,
    output_weight,
    norm_gain,
    block_mask,
):
    latent = latents[0]
    rows, width = latent.shape
    step = lax.axis_index("step")
    frame = lax.axis_index("frame")
    x, core = step // 2, lax.rem(step, 2)
    z, y = frame // NY, lax.rem(frame, NY)
    where_am_i = jnp.stack([step, x, core, frame]).astype(jnp.int32)

    table = jnp.transpose(modulation, (1, 0, 2))

    size_own = step_sizes[step_index[step]]
    size_other = step_sizes[step_index[step + 1 - 2 * core]]

    out_width = output_weight.shape[1]
    two_raw = y_shift(latent, 2)
    packed = jnp.concatenate([input_weight, output_weight.reshape(2, -1)], axis=0)
    packed = jnp.broadcast_to(packed[None], (NZ,) + packed.shape)
    packed, latent = lax.optimization_barrier((packed, latent))
    columns_z = [[NY * i + j for i in range(NZ)] for j in range(NY)]
    column = lax.all_to_all(packed, "frame", 0, 0, axis_index_groups=columns_z)
    column = column.reshape(8 * NZ, -1)
    modulated = modulate(where_am_i, step_index, latent, table)
    column, modulated, two_raw, size_own, size_other = lax.optimization_barrier(
        (column, modulated, two_raw, size_own, size_other)
    )

    zp, zm = z_shift(modulated, 1), z_shift(modulated, -1)
    plane = placed_y([column] + [y_shift(column, -d) for d in range(1, NY)], y)
    plane, zp, zm = lax.optimization_barrier((plane, zp, zm))
    in_rows = plane[:, :, :6].reshape(192, -1)
    out_rows = plane[:, :, 6:].reshape(96, out_width)

    left = x_shift(in_rows, 1)
    zp2, zm2 = z_shift(zp, 1), z_shift(zm, -1)
    before = y_shift(jnp.where(y == NY - 1, zp, modulated), 1)
    after = y_shift(jnp.where(y == 0, zm, modulated), -1)
    two_a = modulate(where_am_i, step_index, two_raw, table)
    in_rows, out_rows, left, zp2, zm2, zp, zm, before, after, two_a = lax.optimization_barrier(
        (in_rows, out_rows, left, zp2, zm2, zp, zm, before, after, two_a)
    )

    right, far = x_shift(in_rows, -1), x_shift(left, 1)
    z4_top = z_shift(zp2[: rows // 2], 2)
    z4_bottom = z_shift(zm2[rows // 2 :], -2)
    two_b = y_shift(jnp.where(y >= 2, zp, zm), 2)
    near = [core_swap(piece) for piece in (in_rows, left)]
    out_rows = jnp.stack([out_rows, core_swap(out_rows)])
    right, far, z4_top, z4_bottom, two_b, out_rows = lax.optimization_barrier(
        (right, far, z4_top, z4_bottom, two_b, out_rows)
    )
    slabs = [modulated, zp, zm, two_a, zp2, zm2, before, after, two_b, z4_top, z4_bottom]
    pieces = [in_rows, left, right, far] + near + [core_swap(right), core_swap(far)]

    out_pieces = [out_rows, x_shift(out_rows, 1), x_shift(out_rows, -1), x_shift(out_rows, 2)]
    keep, send = attend(where_am_i, block_mask, norm_gain, slabs, pieces)

    got = core_swap(send)
    own, other, total = output(
        where_am_i, step_index, step_sizes, keep, got, table, out_pieces
    )
    one = x_later(total, 1)
    three = x_later(total, 3)
    two = x_later(total, 2)
    rest = core_swap(other)
    parts = (2, rows // 2, width)
    near_half = (jnp.arange(2, dtype=jnp.int32) == core)[:, None, None]
    odd = jnp.where(core == 1, size_other, 0.0)
    even = jnp.where(core == 0, size_own, 0.0)
    velocity = jnp.where(near_half, own[None], rest[None])
    inner = jnp.where(near_half, odd * other.astype(F32)[None], 0.0)
    base = anchor.reshape(parts) + inner + size_own * velocity.astype(F32)
    two, velocity, base = lax.optimization_barrier((two, velocity.reshape(rows, width), base))
    sums = one.astype(F32) + two.astype(F32) + three.astype(F32)
    earlier = core_swap((sums + even * own.astype(F32)).astype(BF16))
    one, two, three = lax.optimization_barrier((one, two, three))
    sums = one.astype(F32) + two.astype(F32) + three.astype(F32)
    advanced = base + jnp.where(near_half, sums[None], earlier.astype(F32)[None])
    advanced = advanced.reshape(rows, width)
    return (velocity[None], advanced[None])


def solution(mesh):
    placed = (
        P("step", "frame", None),
        P("frame", None),
        P(),
        P(),
        P(),
        P(("step", "frame"), None),
        P(("step", "frame"), None),
        P(),
        P("frame", None),
    )
    return jax.shard_map(
        on_device,
        mesh=mesh,
        in_specs=placed,
        out_specs=(P("step", "frame", None), P("step", "frame", None)),
        check_vma=False,
    )
```

```python
import functools
import math

import jax
import jax.numpy as jnp
from jax import lax
from jax.experimental import pallas as pl
from jax.experimental.pallas import tpu as pltpu
from jax.sharding import PartitionSpec as P

HD = 128
BLK = 128
NX, NY, NZ = 4, 4, 8
NORM_EPS = 1e-06
F32 = jnp.float32
BF16 = jnp.bfloat16
ATTEND_VMEM = 32 * 1024 * 1024
OUTPUT_VMEM = 16 * 1024 * 1024


def y_shift(block, distance):
    pairs = [(4 * z + y, 4 * z + (y + distance) % NY) for z in range(NZ) for y in range(NY)]
    return lax.ppermute(block, "frame", pairs)


def z_shift(block, distance):
    pairs = [(4 * z + y, 4 * ((z + distance) % NZ) + y) for z in range(NZ) for y in range(NY)]
    return lax.ppermute(block, "frame", pairs)


def x_shift(block, distance):
    pairs = [(2 * x + c, 2 * ((x + distance) % NX) + c) for x in range(NX) for c in range(2)]
    return lax.ppermute(block, "step", pairs)


def x_later(block, distance):
    pairs = [(2 * x + c, 2 * (x + distance) + c) for x in range(NX - distance) for c in range(2)]
    return lax.ppermute(block, "step", pairs)


def core_swap(block):
    return lax.ppermute(block, "step", [(i, i ^ 1) for i in range(2 * NX)])


def modulate_kernel(where_ref, index_ref, latent_ref, table_ref, out_ref, row_s, sem):
    own = index_ref[where_ref[0]]
    copies = [
        pltpu.make_async_copy(table_ref.at[i, pl.ds(own, 1)], row_s.at[i], sem.at[i])
        for i in range(2)
    ]
    for copy in copies:
        copy.start()
    value = latent_ref[...].astype(F32)
    centered = value - jnp.mean(value, axis=-1, keepdims=True)
    variance = jnp.mean(centered * centered, axis=-1, keepdims=True)
    normed = centered * lax.rsqrt(variance + NORM_EPS)
    for copy in copies:
        copy.wait()
    out_ref[...] = (normed * (1.0 + row_s[1]) + row_s[0]).astype(BF16)


def modulate(where, step_index, latent, table):
    rows, width = latent.shape
    return pl.pallas_call(
        modulate_kernel,
        in_specs=[
            pl.BlockSpec(memory_space=pltpu.SMEM),
            pl.BlockSpec(memory_space=pltpu.SMEM),
            pl.BlockSpec(memory_space=pltpu.VMEM),
            pl.BlockSpec(memory_space=pl.ANY),
        ],
        out_specs=pl.BlockSpec(memory_space=pltpu.VMEM),
        out_shape=jax.ShapeDtypeStruct((rows, width), BF16),
        scratch_shapes=[pltpu.VMEM((2, 1, width), F32), pltpu.SemaphoreType.DMA((2,))],
        compiler_params=pltpu.CompilerParams(vmem_limit_bytes=OUTPUT_VMEM),
        name="modulate",
    )(where, step_index, latent, table)


N_SLABS = 10


def attend_kernel(
    where_ref,
    mask_ref,
    gain_ref,
    *refs,
):
    slabs = refs[:9]
    z4_top, z4_bottom = refs[9:11]
    pieces = refs[11:19]
    keep_ref, send_ref = refs[19:21]
    m_s, w_s, k_s, v_s, q_s, bias_s, m_sem, w_sem = refs[21:]
    x, core, frame = where_ref[1], where_ref[2], where_ref[3]
    rows = q_s.shape[0]
    feats = q_s.shape[1]
    half = rows // 2

    copies_m = []
    for i in range(9):
        copies_m.append(pltpu.make_async_copy(slabs[i], m_s.at[pl.ds(i * rows, rows)], m_sem.at[i]))
    copies_m.append(pltpu.make_async_copy(z4_top, m_s.at[pl.ds(9 * rows, half)], m_sem.at[9]))
    copies_m.append(
        pltpu.make_async_copy(z4_bottom, m_s.at[pl.ds(9 * rows + half, half)], m_sem.at[10])
    )
    depth = w_s.shape[0] // (2 * NX)
    copies_w = []
    for who in range(2):
        for i, distance in enumerate((0, -1, 1, 2)):
            piece = pieces[who * 4 + i]
            from_x = lax.rem(x + distance + NX, NX)
            from_core = core if who == 0 else 1 - core
            start = pl.multiple_of((2 * from_x + from_core) * depth, 16)
            copies_w.append(
                pltpu.make_async_copy(
                    piece, w_s.at[pl.ds(start, depth)], w_sem.at[who * 4 + i]
                )
            )
    copies_m[0].start()
    for copy in copies_w:
        copy.start()
    for copy in copies_m[1:]:
        copy.start()

    low = lax.rem(frame, NY) < 2
    two_a = jnp.where(low, 2, -2)
    offsets = (0, -4, 4, two_a, -8, 8, -1, 1, -two_a)
    for i in range(N_SLABS):
        if i < 9:
            source = frame + offsets[i]
        else:
            source = lax.rem(frame + 16, 32)
        inside = jnp.logical_and(source >= 0, source < 32)
        source = jnp.clip(source, 0, 31)
        for q_block in range(2):
            for k_block in range(2):
                ok = jnp.logical_and(inside, mask_ref[q_block, 2 * source + k_block] > 0)
                bias_s[q_block : q_block + 1, pl.ds(i * rows + k_block * BLK, BLK)] = jnp.full(
                    (1, BLK), jnp.where(ok, 0.0, -jnp.inf), F32
                )

    def rms(value, gain):
        square = jnp.mean(value * value, axis=-1, keepdims=True)
        return (value * lax.rsqrt(square + NORM_EPS) * gain).astype(BF16)

    copies_m[0].wait()
    for copy in copies_w:
        copy.wait()
    projected = jnp.dot(m_s[0:rows], w_s[:, 0:feats], preferred_element_type=F32)
    q_s[...] = rms(projected, gain_ref[0:1, :])
    for copy in copies_m[1:]:
        copy.wait()

    span = 2 * rows

    def project(i, carry):
        at = pl.ds(pl.multiple_of(i * span, span), span)
        block = m_s[at]
        keys = jnp.dot(block, w_s[:, feats : 2 * feats], preferred_element_type=F32)
        k_s[at] = rms(keys, gain_ref[1:2, :])
        values = jnp.dot(block, w_s[:, 2 * feats :], preferred_element_type=F32)
        v_s[at] = values.astype(BF16)
        return carry

    lax.fori_loop(0, N_SLABS // 2, project, 0)

    factor = 1.0 / math.sqrt(HD)
    for out_ref, q_block in ((send_ref, 1 - core), (keep_ref, core)):
        at = pl.ds(pl.multiple_of(q_block * BLK, BLK), BLK)
        bias = bias_s[pl.ds(q_block, 1), :]
        for head in range(feats // HD):
            cols = slice(head * HD, (head + 1) * HD)
            scores = lax.dot_general(
                q_s[at, cols], k_s[:, cols], (((1,), (1,)), ((), ())), preferred_element_type=F32
            )
            scores = scores * factor + bias
            peak = jnp.max(scores, axis=-1, keepdims=True)
            terms = jnp.exp(scores - peak)
            total = jnp.sum(terms, axis=-1, keepdims=True)
            mixed = jnp.dot(terms.astype(BF16), v_s[:, cols], preferred_element_type=F32)
            out_ref[:, cols] = (mixed / total).astype(BF16)


def attend(where, block_mask, norm_gain, slabs, pieces):
    rows, width = slabs[0].shape
    feats = norm_gain.shape[1]
    keys = N_SLABS * rows
    any_spec = pl.BlockSpec(memory_space=pl.ANY)
    smem = pl.BlockSpec(memory_space=pltpu.SMEM)
    return pl.pallas_call(
        attend_kernel,
        in_specs=[smem, smem, pl.BlockSpec(memory_space=pltpu.VMEM)]
        + [any_spec] * (len(slabs) + len(pieces)),
        out_specs=[pl.BlockSpec(memory_space=pltpu.VMEM)] * 2,
        out_shape=[jax.ShapeDtypeStruct((BLK, feats), BF16)] * 2,
        scratch_shapes=[
            pltpu.VMEM((keys, width), BF16),
            pltpu.VMEM((width, 3 * feats), BF16),
            pltpu.VMEM((keys, feats), BF16),
            pltpu.VMEM((keys, feats), BF16),
            pltpu.VMEM((rows, feats), BF16),
            pltpu.VMEM((2, keys), F32),
            pltpu.SemaphoreType.DMA((11,)),
            pltpu.SemaphoreType.DMA((8,)),
        ],
        compiler_params=pltpu.CompilerParams(vmem_limit_bytes=ATTEND_VMEM),
        cost_estimate=pl.CostEstimate(
            flops=16_000_000_000, bytes_accessed=16_000_000, transcendentals=4_000_000
        ),
        name="attend",
    )(where, block_mask, norm_gain, *slabs, *pieces)


def output_kernel(where_ref, index_ref, size_ref, keep_ref, got_ref, table_ref, *refs):
    pieces = refs[:4]
    own_ref, other_ref, total_ref, w_s, row_s, sem, row_sem = refs[4:]
    step, x, core = where_ref[0], where_ref[1], where_ref[2]
    own_index = index_ref[step]
    other_index = index_ref[step + 1 - 2 * core]
    depth = w_s.shape[0] // (2 * NX)
    copies = []
    for who in range(2):
        for i, distance in enumerate((0, -1, 1, 2)):
            from_x = lax.rem(x + distance + NX, NX)
            from_core = core if who == 0 else 1 - core
            start = pl.multiple_of((2 * from_x + from_core) * depth, 16)
            copies.append(
                pltpu.make_async_copy(
                    pieces[i].at[who], w_s.at[pl.ds(start, depth)], sem.at[who * 4 + i]
                )
            )
    for i, index in enumerate((own_index, other_index)):
        copies.append(
            pltpu.make_async_copy(table_ref.at[2, pl.ds(index, 1)], row_s.at[i], row_sem.at[i])
        )
    for copy in copies:
        copy.start()
    for copy in copies:
        copy.wait()
    both = jnp.concatenate([keep_ref[...], got_ref[...]], axis=0)
    both = jnp.dot(both, w_s[...], preferred_element_type=F32)
    half = keep_ref.shape[0]
    own = (row_s[0] * both[:half]).astype(BF16)
    other = (row_s[1] * both[half:]).astype(BF16)
    own_ref[...] = own
    other_ref[...] = other
    total_ref[...] = (
        size_ref[own_index] * own.astype(F32) + size_ref[other_index] * other.astype(F32)
    ).astype(BF16)


def output(where, step_index, step_sizes, keep, got, table, pieces):
    half, feats = keep.shape
    width = table.shape[2]
    any_spec = pl.BlockSpec(memory_space=pl.ANY)
    vmem = pl.BlockSpec(memory_space=pltpu.VMEM)
    smem = pl.BlockSpec(memory_space=pltpu.SMEM)
    return pl.pallas_call(
        output_kernel,
        in_specs=[smem, smem, smem, vmem, vmem] + [any_spec] * 5,
        out_specs=[vmem] * 3,
        scratch_shapes=[
            pltpu.VMEM((feats, width), BF16),
            pltpu.VMEM((2, 1, width), F32),
            pltpu.SemaphoreType.DMA((8,)),
            pltpu.SemaphoreType.DMA((2,)),
        ],
        out_shape=[jax.ShapeDtypeStruct((half, width), BF16)] * 3,
        compiler_params=pltpu.CompilerParams(vmem_limit_bytes=OUTPUT_VMEM),
        name="output",
    )(where, step_index, step_sizes, keep, got, table, *pieces)


def placed_y(parts, own):
    result = jnp.zeros((NZ, NY, 8, parts[0].shape[1]), BF16)
    for i, part in enumerate(parts):
        part = part.reshape(NZ, 1, 8, -1)
        result = lax.dynamic_update_slice_in_dim(result, part, lax.rem(own + i, NY), 1)
    return result


def on_device(
    latents,
    anchor,
    step_index,
    modulation,
    step_sizes,
    input_weight,
    output_weight,
    norm_gain,
    block_mask,
):
    latent = latents[0]
    rows, width = latent.shape
    step = lax.axis_index("step")
    frame = lax.axis_index("frame")
    x, core = step // 2, lax.rem(step, 2)
    z, y = frame // NY, lax.rem(frame, NY)
    where_am_i = jnp.stack([step, x, core, frame]).astype(jnp.int32)

    table = jnp.transpose(modulation, (1, 0, 2))

    size_own = step_sizes[step_index[step]]
    size_other = step_sizes[step_index[step + 1 - 2 * core]]

    out_width = output_weight.shape[1]
    two_raw = y_shift(latent, 2)
    packed = jnp.concatenate([input_weight, output_weight.reshape(2, -1)], axis=0)
    packed = jnp.broadcast_to(packed[None], (NZ,) + packed.shape)
    packed, latent = lax.optimization_barrier((packed, latent))
    columns_z = [[NY * i + j for i in range(NZ)] for j in range(NY)]
    column = lax.all_to_all(packed, "frame", 0, 0, axis_index_groups=columns_z)
    column = column.reshape(8 * NZ, -1)
    modulated = modulate(where_am_i, step_index, latent, table)
    column, modulated, two_raw, size_own, size_other = lax.optimization_barrier(
        (column, modulated, two_raw, size_own, size_other)
    )

    zp, zm = z_shift(modulated, 1), z_shift(modulated, -1)
    plane = placed_y([column] + [y_shift(column, -d) for d in range(1, NY)], y)
    plane, zp, zm = lax.optimization_barrier((plane, zp, zm))
    in_rows = plane[:, :, :6].reshape(192, -1)
    out_rows = plane[:, :, 6:].reshape(96, out_width)

    left = x_shift(in_rows, 1)
    zp2, zm2 = z_shift(zp, 1), z_shift(zm, -1)
    before = y_shift(jnp.where(y == NY - 1, zp, modulated), 1)
    after = y_shift(jnp.where(y == 0, zm, modulated), -1)
    two_a = modulate(where_am_i, step_index, two_raw, table)
    in_rows, out_rows, left, zp2, zm2, zp, zm, before, after, two_a = lax.optimization_barrier(
        (in_rows, out_rows, left, zp2, zm2, zp, zm, before, after, two_a)
    )

    right, far = x_shift(in_rows, -1), x_shift(left, 1)
    z4_top = z_shift(zp2[: rows // 2], 2)
    z4_bottom = z_shift(zm2[rows // 2 :], -2)
    two_b = y_shift(jnp.where(y >= 2, zp, zm), 2)
    near = [core_swap(piece) for piece in (in_rows, left)]
    out_rows = jnp.stack([out_rows, core_swap(out_rows)])
    right, far, z4_top, z4_bottom, two_b, out_rows = lax.optimization_barrier(
        (right, far, z4_top, z4_bottom, two_b, out_rows)
    )
    slabs = [modulated, zp, zm, two_a, zp2, zm2, before, after, two_b, z4_top, z4_bottom]
    pieces = [in_rows, left, right, far] + near + [core_swap(right), core_swap(far)]

    out_pieces = [out_rows, x_shift(out_rows, 1), x_shift(out_rows, -1), x_shift(out_rows, 2)]
    keep, send = attend(where_am_i, block_mask, norm_gain, slabs, pieces)

    got = core_swap(send)
    own, other, total = output(
        where_am_i, step_index, step_sizes, keep, got, table, out_pieces
    )
    one = x_later(total, 1)
    three = x_later(total, 3)
    two = x_later(total, 2)
    rest = core_swap(other)
    parts = (2, rows // 2, width)
    near_half = (jnp.arange(2, dtype=jnp.int32) == core)[:, None, None]
    own32 = own.astype(F32)
    velocity = jnp.where(near_half, own[None], rest[None]).reshape(rows, width)
    two, velocity = lax.optimization_barrier((two, velocity))
    even = jnp.where(core == 0, size_own, 0.0)
    odd = jnp.where(core == 1, size_other, 0.0)
    sums = one.astype(F32) + two.astype(F32) + three.astype(F32)
    earlier = core_swap((sums + even * own32).astype(BF16))
    one, two, three, own = lax.optimization_barrier((one, two, three, own))
    sums = one.astype(F32) + two.astype(F32) + three.astype(F32)
    own_part = sums + odd * other.astype(F32) + size_own * own.astype(F32)
    rest_part = earlier.astype(F32) + size_own * rest.astype(F32)
    advanced = anchor.reshape(parts) + jnp.where(near_half, own_part[None], rest_part[None])
    advanced = advanced.reshape(rows, width)
    return (velocity[None], advanced[None])


def solution(mesh):
    placed = (
        P("step", "frame", None),
        P("frame", None),
        P(),
        P(),
        P(),
        P(("step", "frame"), None),
        P(("step", "frame"), None),
        P(),
        P("frame", None),
    )
    return jax.shard_map(
        on_device,
        mesh=mesh,
        in_specs=placed,
        out_specs=(P("step", "frame", None), P("step", "frame", None)),
        check_vma=False,
    )
```

```python
import functools
import math

import jax
import jax.numpy as jnp
from jax import lax
from jax.experimental import pallas as pl
from jax.experimental.pallas import tpu as pltpu
from jax.sharding import PartitionSpec as P

HD = 128
BLK = 128
NX, NY, NZ = 4, 4, 8
NORM_EPS = 1e-06
F32 = jnp.float32
BF16 = jnp.bfloat16
ATTEND_VMEM = 32 * 1024 * 1024
OUTPUT_VMEM = 16 * 1024 * 1024


def y_shift(block, distance):
    pairs = [(4 * z + y, 4 * z + (y + distance) % NY) for z in range(NZ) for y in range(NY)]
    return lax.ppermute(block, "frame", pairs)


def z_shift(block, distance):
    pairs = [(4 * z + y, 4 * ((z + distance) % NZ) + y) for z in range(NZ) for y in range(NY)]
    return lax.ppermute(block, "frame", pairs)


def x_shift(block, distance):
    pairs = [(2 * x + c, 2 * ((x + distance) % NX) + c) for x in range(NX) for c in range(2)]
    return lax.ppermute(block, "step", pairs)


def x_later(block, distance):
    pairs = [(2 * x + c, 2 * (x + distance) + c) for x in range(NX - distance) for c in range(2)]
    return lax.ppermute(block, "step", pairs)


def core_swap(block):
    return lax.ppermute(block, "step", [(i, i ^ 1) for i in range(2 * NX)])


def modulate_kernel(where_ref, index_ref, latent_ref, table_ref, out_ref, row_s, sem):
    own = index_ref[where_ref[0]]
    copies = [
        pltpu.make_async_copy(table_ref.at[i, pl.ds(own, 1)], row_s.at[i], sem.at[i])
        for i in range(2)
    ]
    for copy in copies:
        copy.start()
    value = latent_ref[...].astype(F32)
    centered = value - jnp.mean(value, axis=-1, keepdims=True)
    variance = jnp.mean(centered * centered, axis=-1, keepdims=True)
    normed = centered * lax.rsqrt(variance + NORM_EPS)
    for copy in copies:
        copy.wait()
    out_ref[...] = (normed * (1.0 + row_s[1]) + row_s[0]).astype(BF16)


def modulate(where, step_index, latent, table):
    rows, width = latent.shape
    return pl.pallas_call(
        modulate_kernel,
        in_specs=[
            pl.BlockSpec(memory_space=pltpu.SMEM),
            pl.BlockSpec(memory_space=pltpu.SMEM),
            pl.BlockSpec(memory_space=pltpu.VMEM),
            pl.BlockSpec(memory_space=pl.ANY),
        ],
        out_specs=pl.BlockSpec(memory_space=pltpu.VMEM),
        out_shape=jax.ShapeDtypeStruct((rows, width), BF16),
        scratch_shapes=[pltpu.VMEM((2, 1, width), F32), pltpu.SemaphoreType.DMA((2,))],
        compiler_params=pltpu.CompilerParams(vmem_limit_bytes=OUTPUT_VMEM),
        name="modulate",
    )(where, step_index, latent, table)


N_SLABS = 10


def attend_kernel(
    where_ref,
    mask_ref,
    gain_ref,
    *refs,
):
    slabs = refs[:9]
    z4_top, z4_bottom = refs[9:11]
    pieces = refs[11:19]
    keep_ref, send_ref = refs[19:21]
    m_s, w_s, k_s, v_s, q_s, bias_s, m_sem, w_sem = refs[21:]
    x, core, frame = where_ref[1], where_ref[2], where_ref[3]
    rows = q_s.shape[0]
    feats = q_s.shape[1]
    half = rows // 2

    copies_m = []
    for i in range(9):
        copies_m.append(pltpu.make_async_copy(slabs[i], m_s.at[pl.ds(i * rows, rows)], m_sem.at[i]))
    copies_m.append(pltpu.make_async_copy(z4_top, m_s.at[pl.ds(9 * rows, half)], m_sem.at[9]))
    copies_m.append(
        pltpu.make_async_copy(z4_bottom, m_s.at[pl.ds(9 * rows + half, half)], m_sem.at[10])
    )
    depth = w_s.shape[0] // (2 * NX)
    copies_w = []
    for who in range(2):
        for i, distance in enumerate((0, -1, 1, 2)):
            piece = pieces[who * 4 + i]
            from_x = lax.rem(x + distance + NX, NX)
            from_core = core if who == 0 else 1 - core
            start = pl.multiple_of((2 * from_x + from_core) * depth, 16)
            copies_w.append(
                pltpu.make_async_copy(
                    piece, w_s.at[pl.ds(start, depth)], w_sem.at[who * 4 + i]
                )
            )
    copies_m[0].start()
    for copy in copies_w:
        copy.start()
    for copy in copies_m[1:]:
        copy.start()

    low = lax.rem(frame, NY) < 2
    two_a = jnp.where(low, 2, -2)
    offsets = (0, -4, 4, two_a, -8, 8, -1, 1, -two_a)
    for i in range(N_SLABS):
        if i < 9:
            source = frame + offsets[i]
        else:
            source = lax.rem(frame + 16, 32)
        inside = jnp.logical_and(source >= 0, source < 32)
        source = jnp.clip(source, 0, 31)
        for q_block in range(2):
            for k_block in range(2):
                ok = jnp.logical_and(inside, mask_ref[q_block, 2 * source + k_block] > 0)
                bias_s[q_block : q_block + 1, pl.ds(i * rows + k_block * BLK, BLK)] = jnp.full(
                    (1, BLK), jnp.where(ok, 0.0, -jnp.inf), F32
                )

    def rms(value, gain):
        square = jnp.mean(value * value, axis=-1, keepdims=True)
        return (value * lax.rsqrt(square + NORM_EPS) * gain).astype(BF16)

    copies_m[0].wait()
    for copy in copies_w:
        copy.wait()
    projected = jnp.dot(m_s[0:rows], w_s[:, 0:feats], preferred_element_type=F32)
    q_s[...] = rms(projected, gain_ref[0:1, :])
    for copy in copies_m[1:]:
        copy.wait()

    span = 2 * rows

    def project(i, carry):
        at = pl.ds(pl.multiple_of(i * span, span), span)
        block = m_s[at]
        keys = jnp.dot(block, w_s[:, feats : 2 * feats], preferred_element_type=F32)
        k_s[at] = rms(keys, gain_ref[1:2, :])
        values = jnp.dot(block, w_s[:, 2 * feats :], preferred_element_type=F32)
        v_s[at] = values.astype(BF16)
        return carry

    lax.fori_loop(0, N_SLABS // 2, project, 0)

    factor = 1.0 / math.sqrt(HD)
    for out_ref, q_block in ((send_ref, 1 - core), (keep_ref, core)):
        at = pl.ds(pl.multiple_of(q_block * BLK, BLK), BLK)
        bias = bias_s[pl.ds(q_block, 1), :]
        for head in range(feats // HD):
            cols = slice(head * HD, (head + 1) * HD)
            scores = lax.dot_general(
                q_s[at, cols], k_s[:, cols], (((1,), (1,)), ((), ())), preferred_element_type=F32
            )
            scores = scores * factor + bias
            peak = jnp.max(scores, axis=-1, keepdims=True)
            terms = jnp.exp(scores - peak)
            total = jnp.sum(terms, axis=-1, keepdims=True)
            mixed = jnp.dot(terms.astype(BF16), v_s[:, cols], preferred_element_type=F32)
            out_ref[:, cols] = (mixed / total).astype(BF16)


def attend(where, block_mask, norm_gain, slabs, pieces):
    rows, width = slabs[0].shape
    feats = norm_gain.shape[1]
    keys = N_SLABS * rows
    any_spec = pl.BlockSpec(memory_space=pl.ANY)
    smem = pl.BlockSpec(memory_space=pltpu.SMEM)
    return pl.pallas_call(
        attend_kernel,
        in_specs=[smem, smem, pl.BlockSpec(memory_space=pltpu.VMEM)]
        + [any_spec] * (len(slabs) + len(pieces)),
        out_specs=[pl.BlockSpec(memory_space=pltpu.VMEM)] * 2,
        out_shape=[jax.ShapeDtypeStruct((BLK, feats), BF16)] * 2,
        scratch_shapes=[
            pltpu.VMEM((keys, width), BF16),
            pltpu.VMEM((width, 3 * feats), BF16),
            pltpu.VMEM((keys, feats), BF16),
            pltpu.VMEM((keys, feats), BF16),
            pltpu.VMEM((rows, feats), BF16),
            pltpu.VMEM((2, keys), F32),
            pltpu.SemaphoreType.DMA((11,)),
            pltpu.SemaphoreType.DMA((8,)),
        ],
        compiler_params=pltpu.CompilerParams(vmem_limit_bytes=ATTEND_VMEM),
        cost_estimate=pl.CostEstimate(
            flops=16_000_000_000, bytes_accessed=16_000_000, transcendentals=4_000_000
        ),
        name="attend",
    )(where, block_mask, norm_gain, *slabs, *pieces)


def output_kernel(where_ref, index_ref, size_ref, keep_ref, got_ref, table_ref, *refs):
    pieces = refs[:4]
    own_ref, other_ref, total_ref, w_s, row_s, sem, row_sem = refs[4:]
    step, x, core = where_ref[0], where_ref[1], where_ref[2]
    own_index = index_ref[step]
    other_index = index_ref[step + 1 - 2 * core]
    depth = w_s.shape[0] // (2 * NX)
    copies = []
    for who in range(2):
        for i, distance in enumerate((0, -1, 1, 2)):
            from_x = lax.rem(x + distance + NX, NX)
            from_core = core if who == 0 else 1 - core
            start = pl.multiple_of((2 * from_x + from_core) * depth, 16)
            copies.append(
                pltpu.make_async_copy(
                    pieces[i].at[who], w_s.at[pl.ds(start, depth)], sem.at[who * 4 + i]
                )
            )
    for i, index in enumerate((own_index, other_index)):
        copies.append(
            pltpu.make_async_copy(table_ref.at[2, pl.ds(index, 1)], row_s.at[i], row_sem.at[i])
        )
    for copy in copies:
        copy.start()
    for copy in copies:
        copy.wait()
    both = jnp.concatenate([keep_ref[...], got_ref[...]], axis=0)
    both = jnp.dot(both, w_s[...], preferred_element_type=F32)
    half = keep_ref.shape[0]
    own = (row_s[0] * both[:half]).astype(BF16)
    other = (row_s[1] * both[half:]).astype(BF16)
    own_ref[...] = own
    other_ref[...] = other
    total_ref[...] = (
        size_ref[own_index] * own.astype(F32) + size_ref[other_index] * other.astype(F32)
    ).astype(BF16)


def output(where, step_index, step_sizes, keep, got, table, pieces):
    half, feats = keep.shape
    width = table.shape[2]
    any_spec = pl.BlockSpec(memory_space=pl.ANY)
    vmem = pl.BlockSpec(memory_space=pltpu.VMEM)
    smem = pl.BlockSpec(memory_space=pltpu.SMEM)
    return pl.pallas_call(
        output_kernel,
        in_specs=[smem, smem, smem, vmem, vmem] + [any_spec] * 5,
        out_specs=[vmem] * 3,
        scratch_shapes=[
            pltpu.VMEM((feats, width), BF16),
            pltpu.VMEM((2, 1, width), F32),
            pltpu.SemaphoreType.DMA((8,)),
            pltpu.SemaphoreType.DMA((2,)),
        ],
        out_shape=[jax.ShapeDtypeStruct((half, width), BF16)] * 3,
        compiler_params=pltpu.CompilerParams(vmem_limit_bytes=OUTPUT_VMEM),
        name="output",
    )(where, step_index, step_sizes, keep, got, table, *pieces)


def placed_y(parts, own):
    result = jnp.zeros((NZ, NY, 8, parts[0].shape[1]), BF16)
    for i, part in enumerate(parts):
        part = part.reshape(NZ, 1, 8, -1)
        result = lax.dynamic_update_slice_in_dim(result, part, lax.rem(own + i, NY), 1)
    return result


def on_device(
    latents,
    anchor,
    step_index,
    modulation,
    step_sizes,
    input_weight,
    output_weight,
    norm_gain,
    block_mask,
):
    latent = latents[0]
    rows, width = latent.shape
    step = lax.axis_index("step")
    frame = lax.axis_index("frame")
    x, core = step // 2, lax.rem(step, 2)
    z, y = frame // NY, lax.rem(frame, NY)
    where_am_i = jnp.stack([step, x, core, frame]).astype(jnp.int32)

    table = jnp.transpose(modulation, (1, 0, 2))

    size_own = step_sizes[step_index[step]]
    size_other = step_sizes[step_index[step + 1 - 2 * core]]

    out_width = output_weight.shape[1]
    two_raw = y_shift(latent, 2)
    packed = jnp.concatenate([input_weight, output_weight.reshape(2, -1)], axis=0)
    packed = jnp.broadcast_to(packed[None], (NZ,) + packed.shape)
    packed, latent = lax.optimization_barrier((packed, latent))
    columns_z = [[NY * i + j for i in range(NZ)] for j in range(NY)]
    column = lax.all_to_all(packed, "frame", 0, 0, axis_index_groups=columns_z)
    column = column.reshape(8 * NZ, -1)
    modulated = modulate(where_am_i, step_index, latent, table)
    column, modulated, two_raw, size_own, size_other = lax.optimization_barrier(
        (column, modulated, two_raw, size_own, size_other)
    )

    zp, zm = z_shift(modulated, 1), z_shift(modulated, -1)
    plane = placed_y([column] + [y_shift(column, -d) for d in range(1, NY)], y)
    plane, zp, zm = lax.optimization_barrier((plane, zp, zm))
    in_rows = plane[:, :, :6].reshape(192, -1)
    out_rows = plane[:, :, 6:].reshape(96, out_width)

    left = x_shift(in_rows, 1)
    zp2, zm2 = z_shift(zp, 1), z_shift(zm, -1)
    before = y_shift(jnp.where(y == NY - 1, zp, modulated), 1)
    after = y_shift(jnp.where(y == 0, zm, modulated), -1)
    two_a = modulate(where_am_i, step_index, two_raw, table)
    in_rows, out_rows, left, zp2, zm2, zp, zm, before, after, two_a = lax.optimization_barrier(
        (in_rows, out_rows, left, zp2, zm2, zp, zm, before, after, two_a)
    )

    right, far = x_shift(in_rows, -1), x_shift(left, 1)
    z4_top = z_shift(zp2[: rows // 2], 2)
    z4_bottom = z_shift(zm2[rows // 2 :], -2)
    two_b = y_shift(jnp.where(y >= 2, zp, zm), 2)
    near = [core_swap(piece) for piece in (in_rows, left)]
    out_rows = jnp.stack([out_rows, core_swap(out_rows)])
    right, far, z4_top, z4_bottom, two_b, out_rows = lax.optimization_barrier(
        (right, far, z4_top, z4_bottom, two_b, out_rows)
    )
    slabs = [modulated, zp, zm, two_a, zp2, zm2, before, after, two_b, z4_top, z4_bottom]
    pieces = [in_rows, left, right, far] + near + [core_swap(right), core_swap(far)]

    out_pieces = [out_rows, x_shift(out_rows, 1), x_shift(out_rows, -1), x_shift(out_rows, 2)]
    keep, send = attend(where_am_i, block_mask, norm_gain, slabs, pieces)

    got = core_swap(send)
    own, other, total = output(
        where_am_i, step_index, step_sizes, keep, got, table, out_pieces
    )
    one = x_later(total, 1)
    three = x_later(total, 3)
    two = x_later(total, 2)
    rest = core_swap(other)
    parts = (2, rows // 2, width)
    near_half = (jnp.arange(2, dtype=jnp.int32) == core)[:, None, None]
    own32 = own.astype(F32)
    velocity = jnp.where(near_half, own[None], rest[None]).reshape(rows, width)
    rest_part = size_own * rest.astype(F32)
    two, velocity, rest_part = lax.optimization_barrier((two, velocity, rest_part))
    even = jnp.where(core == 0, size_own, 0.0)
    odd = jnp.where(core == 1, size_other, 0.0)
    sums = one.astype(F32) + two.astype(F32) + three.astype(F32)
    earlier = core_swap((sums + even * own32).astype(BF16))
    one, two, three, own = lax.optimization_barrier((one, two, three, own))
    sums = one.astype(F32) + two.astype(F32) + three.astype(F32)
    own_part = sums + odd * other.astype(F32) + size_own * own.astype(F32)
    rest_part = earlier.astype(F32) + rest_part
    advanced = anchor.reshape(parts) + jnp.where(near_half, own_part[None], rest_part[None])
    advanced = advanced.reshape(rows, width)
    return (velocity[None], advanced[None])


def solution(mesh):
    placed = (
        P("step", "frame", None),
        P("frame", None),
        P(),
        P(),
        P(),
        P(("step", "frame"), None),
        P(("step", "frame"), None),
        P(),
        P("frame", None),
    )
    return jax.shard_map(
        on_device,
        mesh=mesh,
        in_specs=placed,
        out_specs=(P("step", "frame", None), P("step", "frame", None)),
        check_vma=False,
    )
```
